256 devices in a mesh: dp: 64 (over y, z, core), fsdp: 4 (over x).
Axes of the slice: x: 4, y: 4, z: 8, core: 2. Of those that a mesh axis runs over, the one named last changes fastest.
Arguments:
- tokens: bfloat16 [32768, 4096], P('dp', 'fsdp'), may hold values from -6 to 6
- query_weight: bfloat16 [4096, 2048], P('fsdp'), may hold values from -0.09375 to 0.09375
- neighbour_store: bfloat16 [512, 48, 32, 128], P('dp', None, 'fsdp'), may hold values from -170 to 170
- neighbours: int32 [512, 2], replicated, may hold values from 0 to 511, as said below
- attended_grad: bfloat16 [32768, 2048], P('dp', 'fsdp'), may hold values from -16 to 16
Outputs:
- attended: bfloat16 [32768, 2048], P('dp', 'fsdp')
- token_grad: bfloat16 [32768, 4096], P('dp', 'fsdp')
- weight_grad: float32 [4096, 2048], P('fsdp', 'dp')
- store_grad: float32 [512, 48, 32, 128], P('dp', None, 'fsdp')
The draws below stay inside these ranges and needn't reach their ends.
Inputs may be any that keep to these rules, and one draw needn't show every extreme that they name: Entry e lies on store shard e // 8. Among the neighbours of the 8 spans of one index of dp, at most 1 lie on one shard, and some shard holds exactly 1.
All inputs are finite; a program needn't handle non-finite values.
Results may differ from the reference program's by a relative error of at most 0.028.
The reference program's roundings to bfloat16 on the way count: a program that leaves them out, or rounds other values in their place, can miss the bound.
Values may be sent and summed in bfloat16 or wider, within the bound.
A program may use at most 128 MiB of HBM per device.

```python
import math
import jax
import jax.numpy as jnp
from jax import lax

D = 4096
H = 32
DH = 64
SPAN = 64
NEIGH = 2
NB_LEN = 48
CH_GRP = 8
ENTRIES_PER_DATA = 8
HD = 2048
SPANS = 512
TOKENS = 32768
ENTRIES = 512


def draw_neighbours(key, part):
    key = jax.random.fold_in(key, 11)
    partition_sequence = ENTRIES // ENTRIES_PER_DATA
    team_members = SPANS // CH_GRP
    ref_count = CH_GRP * NEIGH
    lookup_indicator, lookup_energies, key_perm, key_entry = jax.random.split(key, 4)
    energy_increment = jnp.where(jax.random.randint(lookup_indicator, (partition_sequence,), 0, 8) == 0, 48, 0)
    match_strength = jax.random.randint(lookup_energies, (team_members, partition_sequence), 0, 64) + energy_increment[None, :]
    order_key = match_strength * partition_sequence + jnp.arange(partition_sequence, dtype=jnp.int32)[None, :]
    ranked = jnp.argsort(-order_key, axis=1).astype(jnp.int32)
    perm_keys = jax.random.split(key_perm, team_members)
    perms = jax.vmap(lambda one_key: jax.random.permutation(one_key, ref_count))(perm_keys)
    picks = (perms % partition_sequence).astype(jnp.int32)
    owners = jnp.take_along_axis(ranked, picks, axis=1)
    local_entry = jax.random.randint(key_entry, (team_members, ref_count), 0, ENTRIES_PER_DATA)
    return (owners * ENTRIES_PER_DATA + local_entry).reshape(SPANS, NEIGH).astype(jnp.int32)


def draw_neighbour_store(key, part):
    key = jax.random.fold_in(key, 5)
    key_base = jax.random.fold_in(key, 0)
    base = jnp.clip(jax.random.normal(key_base, (ENTRIES, NB_LEN, H, 2 * DH), jnp.float32), -4.0, 4.0)
    return base.astype(jnp.bfloat16)


def spiked(array, own_key, source, target, blocks, factor):
    def block_of(position):
        return (jnp.arange(array.shape[position]) // (array.shape[position] // blocks)).reshape((-1,) + (1,) * (array.ndim - 1 - position))

    near = jax.random.permutation(own_key, blocks)[block_of(target)]
    second = (block_of(target) + blocks // 2) % blocks
    return jnp.where((block_of(source) == near) | (block_of(source) == second), factor * array, array)


def steps_of(stream_key, dims, pieces, low, top_value):
    factor_of, own = 1.0, jax.random.fold_in(stream_key, 6)
    for position, shards_of in pieces:
        draws = jnp.exp(jax.random.uniform(jax.random.fold_in(own, position), (shards_of,), jnp.float32, low / len(pieces), top_value / len(pieces)))
        factor_of = factor_of * jnp.repeat(draws, dims[position] // shards_of).reshape([-1 if axis == position else 1 for axis in range(len(dims))])
    return factor_of


def noise(key, extent, spread, reach, cuts=(), kind=jnp.bfloat16):
    loudness = steps_of(key, extent, cuts, -0.22, 0.18) if cuts else 1.0
    entries = jax.random.normal(key, extent, jnp.float32) * spread * loudness
    return jnp.minimum(jnp.maximum(entries, -reach), reach).astype(kind)


def bell_draw_with(key, extent, deviation, reach, shards, heavy, kind=jnp.bfloat16):
    values = deviation * jax.random.normal(key, extent, jnp.float32)
    if shards:
        values = values * steps_of(key, extent, shards, -0.22, 0.18)
    return jnp.clip(spiked(values, jax.random.fold_in(key, 3), *heavy), -reach, reach).astype(kind)


def setup_inputs(seed: int = 0) -> dict:
    streams_of = jax.random.split(jax.random.key(seed), 6)
    return {
        "tokens": noise(streams_of[0], (TOKENS, D), 1.0, 6.0, ((0, 64), (1, 4))),
        "query_weight": noise(streams_of[1], (D, HD), D ** -0.5, 0.09375, ((0, 4),)),
        "neighbour_store": draw_neighbour_store(jax.random.fold_in(streams_of[5], 71), 0),
        "neighbours": draw_neighbours(jax.random.fold_in(streams_of[5], 71), 0),
        "attended_grad": bell_draw_with(streams_of[4], (TOKENS, HD), 1.0, 16.0, ((0, 64), (1, 4)), (0, 1, 64, 4.0)),
    }


def reference(tokens, query_weight, neighbour_store, neighbours, attended_grad):
    inverse_root = 1.0 / math.sqrt(DH)
    queries = jnp.dot(tokens, query_weight, preferred_element_type=jnp.float32).astype(jnp.bfloat16)
    queries = lax.optimization_barrier(queries)
    brought_rows = jnp.take(neighbour_store, neighbours.reshape(-1).astype(jnp.int32), axis=0)
    brought_rows = brought_rows.reshape(SPANS, NEIGH * NB_LEN, H, 2 * DH)
    key_rows = brought_rows[..., :DH].astype(jnp.float32)
    value_rows = brought_rows[..., DH:].astype(jnp.float32)
    query_blocks = queries.reshape(SPANS, SPAN, H, DH).astype(jnp.float32)
    score_raw = jnp.einsum('cqhd,ckhd->chqk', query_blocks, key_rows) * inverse_root
    row_peak = lax.optimization_barrier(jnp.max(score_raw, axis=-1, keepdims=True))
    weights = jnp.exp(score_raw - row_peak)
    softmax_probs = weights / lax.optimization_barrier(jnp.sum(weights, axis=-1, keepdims=True))
    probs_low = lax.optimization_barrier(softmax_probs.astype(jnp.bfloat16)).astype(jnp.float32)
    attended = jnp.einsum('chqk,ckhd->cqhd', probs_low, value_rows)
    attended = attended.astype(jnp.bfloat16).reshape(TOKENS, H * DH)
    grad_blocks = attended_grad.reshape(SPANS, SPAN, H, DH).astype(jnp.float32)
    prob_grad = jnp.einsum('cqhd,ckhd->chqk', grad_blocks, value_rows)
    row_terms = lax.optimization_barrier(jnp.sum(softmax_probs * prob_grad, axis=-1, keepdims=True))
    score_grad = (softmax_probs * (prob_grad - row_terms)).astype(jnp.bfloat16)
    score_grad = lax.optimization_barrier(score_grad).astype(jnp.float32)
    query_grad = (jnp.einsum('chqk,ckhd->cqhd', score_grad, key_rows) * inverse_root).astype(jnp.bfloat16)
    key_grad = jnp.einsum('chqk,cqhd->ckhd', score_grad, query_blocks) * inverse_root
    value_grad = jnp.einsum('chqk,cqhd->ckhd', probs_low, grad_blocks)
    block_grad = jnp.concatenate([key_grad, value_grad], axis=-1).astype(jnp.bfloat16)
    block_grad = block_grad.reshape(SPANS * NEIGH, NB_LEN, H, 2 * DH)
    store_grad = jnp.zeros((ENTRIES, NB_LEN, H, 2 * DH), jnp.float32)
    store_grad = store_grad.at[neighbours.reshape(-1).astype(jnp.int32)].add(block_grad.astype(jnp.float32))
    query_flat = query_grad.reshape(TOKENS, H * DH)
    token_grad = jnp.dot(query_flat, query_weight.T, preferred_element_type=jnp.float32).astype(jnp.bfloat16)
    weight_grad = jnp.dot(tokens.T, query_flat, preferred_element_type=jnp.float32)
    return (attended, token_grad, weight_grad, store_grad)
```

```python
import functools
import math

import jax
import jax.numpy as jnp
from jax import lax
from jax.experimental import pallas as pl
from jax.experimental.pallas import tpu as pltpu
from jax.sharding import PartitionSpec as P

SPAN = 64
NY, NZ = 4, 8
MESH = pl.DeviceIdType.MESH
Z_OFF = (0, -1, 1, -2, 2, -3, 3, 4)
J_OFF = ((0, 0), (0, 1), (-1, 0), (-1, 1), (1, 0), (1, 1), (2, 0), (2, 1))
VMEM_LIMIT = 56 * 1024 * 1024


def dp_of(y, z, c):
    return (y * NZ + z) * 2 + c


def exchange_kernel(by_target, code_ref, own, out, zp0, zp1, zp2, zm0, zm1, zm2, z4, sbuf, rl,
                    zs, zr, ysend, yrecv, rs, rr, fs, ls):
    me = lax.axis_index("dp")
    fs_id = lax.axis_index("fsdp")
    y, z, c = me // (2 * NZ), (me // 2) % NZ, me % 2
    half = own.shape[0] // 2

    def dev(dy, dz, dc):
        cc = c if dc == 0 else 1 - c
        return (dp_of((y + dy + NY) % NY, (z + dz + NZ) % NZ, cc), fs_id)

    greet = [dev(0, 1, 0), dev(0, -1, 0), dev(0, 0, 1),
             dev(1, 0, 0), dev(1, 0, 1), dev(-1, 0, 0), dev(-1, 0, 1)]
    barrier = pltpu.get_barrier_semaphore()
    for d in greet:
        pl.semaphore_signal(barrier, inc=1, device_id=d, device_id_type=MESH)
    pl.semaphore_wait(barrier, len(greet))

    def remote(src, dst, ssem, rsem, d):
        return pltpu.make_async_remote_copy(
            src_ref=src, dst_ref=dst, send_sem=ssem, recv_sem=rsem, device_id=d, device_id_type=MESH)

    up, down = dev(0, 1, 0), dev(0, -1, 0)
    zp, zm = [zp0, zp1, zp2], [zm0, zm1, zm2]
    ups = [remote(own, zp0, zs.at[0], zr.at[0], up),
           remote(zp0, zp1, zs.at[1], zr.at[1], up),
           remote(zp1, zp2, zs.at[2], zr.at[2], up),
           remote(zp2.at[pl.ds(0, half)], z4.at[pl.ds(0, half)], zs.at[3], zr.at[3], up)]
    downs = [remote(own, zm0, zs.at[4], zr.at[4], down),
             remote(zm0, zm1, zs.at[5], zr.at[5], down),
             remote(zm1, zm2, zs.at[6], zr.at[6], down),
             remote(zm2.at[pl.ds(half, half)], z4.at[pl.ds(half, half)], zs.at[7], zr.at[7], down)]
    sets = [own, zp0, zm0, zp1, zm1, zp2, zm2, z4]
    locals_, sends, relays, forwards = [], [], [], []

    def process(k):
        origin = dp_of(y, (z + Z_OFF[k] + NZ) % NZ, c)
        for i, (dy, dc) in enumerate(J_OFF):
            target = dev(dy, 0, dc)[0]
            place = origin * 64 + target if by_target else target * 64 + origin
            code = code_ref[place]
            pick = (code // 8) % 16 if by_target else code % 8
            sbuf[k, i] = sets[k][pick]
        cp = pltpu.make_async_copy(sbuf.at[k, 0], out.at[k], ls.at[k])
        cp.start()
        locals_.append(cp)
        for i, j in ((1, 1), (4, 2), (5, 3), (2, 4), (3, 5)):
            dy, dc = J_OFF[i]
            cp = remote(sbuf.at[k, i], out.at[j * 8 + k], ysend.at[k, i], yrecv.at[j * 8 + k], dev(dy, 0, dc))
            cp.start()
            sends.append(cp)
        cp = remote(sbuf.at[k, pl.ds(6, 2)], rl.at[k], rs.at[k], rr.at[k], dev(1 if k % 2 == 0 else -1, 0, 0))
        cp.start()
        relays.append(cp)

    def relay(k):
        relays[k].wait_recv()
        for dc in range(2):
            cp = remote(rl.at[k, dc], out.at[(6 + dc) * 8 + k], fs.at[k, dc], yrecv.at[(6 + dc) * 8 + k],
                        dev(1 if k % 2 == 0 else -1, 0, dc))
            cp.start()
            forwards.append(cp)

    ups[0].start()
    downs[0].start()
    process(0)
    for s in range(3):
        ups[s].wait_recv()
        ups[s + 1].start()
        downs[s].wait_recv()
        downs[s + 1].start()
        process(1 + 2 * s)
        process(2 + 2 * s)
        if s == 1:
            relay(0)
        if s == 2:
            relay(1)
            relay(2)
    ups[3].wait_recv()
    downs[3].wait_recv()
    process(7)
    for k in range(3, 8):
        relay(k)
    for cp in locals_:
        cp.wait()
    for cp in sends:
        cp.wait()
    for cp in forwards:
        cp.wait()
    for cp in relays + ups + downs:
        cp.wait_send()


def exchange(code, own, by_target, collective_id):
    n, rows, cols = own.shape
    blocks = pltpu.VMEM((n, rows, cols), own.dtype)
    dma = pltpu.SemaphoreType.DMA
    moved = 64 * rows * cols * 2
    return pl.pallas_call(
        functools.partial(exchange_kernel, by_target),
        out_shape=jax.ShapeDtypeStruct((64, rows, cols), own.dtype),
        in_specs=[pl.BlockSpec(memory_space=pltpu.SMEM), pl.BlockSpec(memory_space=pltpu.VMEM)],
        out_specs=pl.BlockSpec(memory_space=pl.ANY),
        scratch_shapes=[blocks] * 7 + [
            pltpu.VMEM((8, 8, rows, cols), own.dtype),
            pltpu.VMEM((8, 2, rows, cols), own.dtype),
            dma((8,)), dma((8,)), dma((8, 8)), dma((64,)), dma((8,)), dma((8,)), dma((8, 2)), dma((8,)),
        ],
        compiler_params=pltpu.CompilerParams(
            collective_id=collective_id, has_side_effects=True, vmem_limit_bytes=VMEM_LIMIT),
        cost_estimate=pl.CostEstimate(flops=0, bytes_accessed=40 * moved, transcendentals=0),
        name="exchange_back" if by_target else "exchange_out",
    )(code, own)


def attention_kernel(pos_ref, q_ref, g_ref, kv0_ref, kv1_ref, att_ref, qg_ref, bg_ref):
    heads = kv0_ref.shape[1]
    width = q_ref.shape[1] // heads
    near = kv0_ref.shape[2]
    root = 1.0 / math.sqrt(width)
    zero = jnp.zeros((SPAN, width), jnp.bfloat16)
    nt = (((1,), (1,)), ((), ()))
    nn = (((1,), (0,)), ((), ()))
    tn = (((0,), (0,)), ((), ()))

    def dot(a, b, dims):
        return lax.dot_general(a, b, dims, preferred_element_type=jnp.float32)

    for h in range(heads):
        cols = slice(h * width, (h + 1) * width)
        q, g = q_ref[:, cols], g_ref[:, cols]
        kv = jnp.concatenate([kv0_ref[0, h], kv1_ref[0, h]], axis=0)
        both = jnp.concatenate(
            [jnp.concatenate([q, zero], axis=1), jnp.concatenate([zero, g], axis=1)], axis=0)
        raw = dot(both, kv, nt)
        score = raw[:SPAN] * root
        prob_grad = raw[SPAN:]
        weights = jnp.exp(score - jnp.max(score, axis=-1, keepdims=True))
        probs = weights / jnp.sum(weights, axis=-1, keepdims=True)
        low = probs.astype(jnp.bfloat16)
        term = jnp.sum(probs * prob_grad, axis=-1, keepdims=True)
        sg = (probs * (prob_grad - term)).astype(jnp.bfloat16)
        applied = dot(jnp.concatenate([low, sg], axis=0), kv, nn)
        att_ref[:, cols] = applied[:SPAN, width:].astype(jnp.bfloat16)
        qg_ref[:, cols] = (applied[SPAN:, :width] * root).astype(jnp.bfloat16)
        back = dot(jnp.concatenate([sg, low], axis=0), both, tn)
        lane = lax.broadcasted_iota(jnp.int32, back.shape, 1)
        back = (back * jnp.where(lane < width, root, 1.0)).astype(jnp.bfloat16)
        bg_ref[0, h] = back[:near]
        bg_ref[1, h] = back[near:]


def attention(pos, queries, grads, blocks):
    rows, cols = queries.shape
    spans = rows // SPAN
    _, heads, near, pair = blocks.shape
    kv = lambda n: pl.BlockSpec((1, heads, near, pair), lambda i, pos: (pos[2 * i + n], 0, 0, 0))
    flat = pl.BlockSpec((SPAN, cols), lambda i, pos: (i, 0))
    return pl.pallas_call(
        attention_kernel,
        grid_spec=pltpu.PrefetchScalarGridSpec(
            num_scalar_prefetch=1,
            grid=(spans,),
            in_specs=[flat, flat, kv(0), kv(1)],
            out_specs=[flat, flat, pl.BlockSpec((2, heads, near, pair), lambda i, pos: (i, 0, 0, 0))],
        ),
        out_shape=[
            jax.ShapeDtypeStruct((rows, cols), jnp.bfloat16),
            jax.ShapeDtypeStruct((rows, cols), jnp.bfloat16),
            jax.ShapeDtypeStruct((2 * spans, heads, near, pair), jnp.bfloat16),
        ],
        compiler_params=pltpu.CompilerParams(vmem_limit_bytes=VMEM_LIMIT),
        name="attention",
    )(pos, queries, grads, blocks, blocks)


def gather_sum_kernel(code_ref, blk_ref, out_ref, acc):
    h = pl.program_id(0)
    acc[...] = jnp.zeros_like(acc)

    def body(i, carry):
        code = code_ref[i]

        @pl.when(code >= 128)
        def _():
            e = code % 8
            acc[e] += blk_ref[i, 0].astype(jnp.float32)

        return carry

    lax.fori_loop(0, 64, body, 0)
    out_ref[0] = acc[...]


def gather_sum(codes, blocks):
    _, heads, near, pair = blocks.shape
    return pl.pallas_call(
        gather_sum_kernel,
        grid=(heads,),
        in_specs=[
            pl.BlockSpec(memory_space=pltpu.SMEM),
            pl.BlockSpec((64, 1, near, pair), lambda h: (0, h, 0, 0)),
        ],
        out_specs=pl.BlockSpec((1, 8, near, pair), lambda h: (h, 0, 0, 0)),
        out_shape=jax.ShapeDtypeStruct((heads, 8, near, pair), jnp.float32),
        scratch_shapes=[pltpu.VMEM((8, near, pair), jnp.float32)],
        compiler_params=pltpu.CompilerParams(vmem_limit_bytes=VMEM_LIMIT),
        name="gather_sum",
    )(codes, blocks)


def slot_devices(me):
    y, z, c = me // (2 * NZ), (me // 2) % NZ, me % 2
    ys = jnp.array([j[0] for j in J_OFF], jnp.int32)[:, None]
    cs = jnp.array([j[1] for j in J_OFF], jnp.int32)[:, None]
    zs = jnp.array(Z_OFF, jnp.int32)[None, :]
    return dp_of((y + ys + NY) % NY, (z + zs + NZ) % NZ, (c + cs) % 2).reshape(-1)


def on_device(tokens, query_weight, neighbour_store, neighbours, attended_grad):
    entries_here, near, heads, pair = neighbour_store.shape
    me = lax.axis_index("dp")
    fields = lax.psum_scatter(
        lax.dot_general(
            query_weight, tokens, (((0,), (1,)), ((), ())), preferred_element_type=jnp.float32
        ),
        "fsdp",
        scatter_dimension=0,
        tiled=True,
    )
    queries = fields.T.astype(jnp.bfloat16)

    refs = neighbours.reshape(64, -1)
    order = jnp.arange(refs.shape[1], dtype=jnp.int32)[None, :]
    word = 128 + 8 * order + refs % entries_here
    shard = jnp.arange(64, dtype=jnp.int32)
    table = jnp.max(
        jnp.where((refs // entries_here)[:, :, None] == shard, word[:, :, None], 0), axis=1)
    code = table.reshape(-1)

    slots = slot_devices(me)
    mine = lax.dynamic_index_in_dim(refs, me, 0, keepdims=False) // entries_here
    pos = jnp.sum(
        jnp.where(mine[:, None] == slots[None, :], jnp.arange(64, dtype=jnp.int32)[None, :], 0), axis=1)

    store = neighbour_store.transpose(0, 2, 1, 3).reshape(entries_here, heads * near, pair)
    got = exchange(code, store, False, 0).reshape(64, heads, near, pair)
    attended, query_grad, block_grad = attention(pos, queries, attended_grad, got)

    full_grad = lax.all_gather(query_grad, "fsdp", axis=1, tiled=True)
    token_grad = lax.dot_general(
        full_grad, query_weight, (((1,), (1,)), ((), ())), preferred_element_type=jnp.float32
    ).astype(jnp.bfloat16)
    weight_share = lax.psum_scatter(
        lax.dot_general(
            full_grad, tokens, (((0,), (0,)), ((), ())), preferred_element_type=jnp.float32
        ),
        "dp",
        scatter_dimension=0,
        tiled=True,
    )
    weight_grad = weight_share.T

    back = exchange(code, block_grad.reshape(-1, heads * near, pair), True, 1)
    column = jnp.take(table, slots, axis=0)
    column = lax.dynamic_index_in_dim(column, me, 1, keepdims=False)
    summed = gather_sum(column, back.reshape(64, heads, near, pair))
    store_grad = summed.transpose(1, 2, 0, 3)
    return (attended, token_grad, weight_grad, store_grad)


def solution(mesh):
    return jax.shard_map(
        on_device,
        mesh=mesh,
        in_specs=(
            P("dp", "fsdp"),
            P("fsdp", None),
            P("dp", None, "fsdp", None),
            P(),
            P("dp", "fsdp"),
        ),
        out_specs=(P("dp", "fsdp"), P("dp", "fsdp"), P("fsdp", "dp"), P("dp", None, "fsdp", None)),
        check_vma=False,
    )
```

```python
import functools
import math

import jax
import jax.numpy as jnp
from jax import lax
from jax.experimental import pallas as pl
from jax.experimental.pallas import tpu as pltpu
from jax.sharding import PartitionSpec as P

SPAN = 64
NY, NZ = 4, 8
MESH = pl.DeviceIdType.MESH
Z_OFF = (0, -1, 1, -2, 2, -3, 3, 4)
J_OFF = ((0, 0), (0, 1), (-1, 0), (-1, 1), (1, 0), (1, 1), (2, 0), (2, 1))
VMEM_LIMIT = 60 * 1024 * 1024


def dp_of(y, z, c):
    return (y * NZ + z) * 2 + c


class Place:
    def __init__(self):
        me = lax.axis_index("dp")
        self.x = lax.axis_index("fsdp")
        self.y, self.z, self.c = me // (2 * NZ), (me // 2) % NZ, me % 2

    def dp(self, dy, dz, dc):
        return dp_of((self.y + dy + NY) % NY, (self.z + dz + NZ) % NZ, (self.c + dc) % 2)

    def dev(self, dy=0, dz=0, dc=0, dx=0):
        return (self.dp(dy, dz, dc), (self.x + dx + 4) % 4)


def greet(devices):
    barrier = pltpu.get_barrier_semaphore()
    for d in devices:
        pl.semaphore_signal(barrier, inc=1, device_id=d, device_id_type=MESH)
    pl.semaphore_wait(barrier, len(devices))


def remote(src, dst, ssem, rsem, d):
    return pltpu.make_async_remote_copy(
        src_ref=src, dst_ref=dst, send_sem=ssem, recv_sem=rsem, device_id=d, device_id_type=MESH)


def plane_partners(p):
    return [p.dev(dy, 0, dc) for dy, dc in J_OFF[1:]]


def plane_send(p, out, k, hh, blocks, ysend, yrecv, ls):
    local = pltpu.make_async_copy(blocks(0), out.at[k, hh], ls.at[k, hh])
    local.start()
    sends = []
    for i, j in ((1, 1), (6, 6), (7, 7), (4, 2), (5, 3), (2, 4), (3, 5)):
        dy, dc = J_OFF[i]
        cp = remote(blocks(i), out.at[j * 8 + k, hh], ysend.at[k, hh, i], yrecv.at[j * 8 + k, hh],
                    p.dev(dy, 0, dc))
        cp.start()
        sends.append(cp)
    return local, sends


def out_kernel(code_ref, own, out, zp0, zp1, zp2, zm0, zm1, zm2, z4, sbuf,
               zs, zr, ysend, yrecv, ls):
    p = Place()
    half = own.shape[0] // 2
    up, down = p.dev(0, 1), p.dev(0, -1)
    greet([up, down] + plane_partners(p))
    zp, zm = [zp0, zp1, zp2], [zm0, zm1, zm2]
    lo, hi = pl.ds(0, half), pl.ds(half, half)
    ups, downs = [], []
    for hh in range(2):
        ups.append([remote(own.at[:, hh], zp0[hh], zs.at[0, hh], zr.at[0, hh], up),
                    remote(zp0[hh], zp1[hh], zs.at[1, hh], zr.at[1, hh], up),
                    remote(zp1[hh], zp2[hh], zs.at[2, hh], zr.at[2, hh], up),
                    remote(zp2[hh].at[lo], z4[hh].at[lo], zs.at[3, hh], zr.at[3, hh], up)])
        downs.append([remote(own.at[:, hh], zm0[hh], zs.at[4, hh], zr.at[4, hh], down),
                      remote(zm0[hh], zm1[hh], zs.at[5, hh], zr.at[5, hh], down),
                      remote(zm1[hh], zm2[hh], zs.at[6, hh], zr.at[6, hh], down),
                      remote(zm2[hh].at[hi], z4[hh].at[hi], zs.at[7, hh], zr.at[7, hh], down)])
    sets = [None, zp0, zm0, zp1, zm1, zp2, zm2, z4]
    started = []

    def process(k, hh):
        origin = p.dp(0, Z_OFF[k], 0)
        for i, (dy, dc) in enumerate(J_OFF):
            pick = code_ref[p.dp(dy, 0, dc) * 64 + origin] % 8
            sbuf[k, hh, i] = own[pick, hh] if k == 0 else sets[k][hh][pick]
        started.append(plane_send(p, out, k, hh, lambda i: sbuf.at[k, hh, i], ysend, yrecv, ls))

    for hh in range(2):
        ups[hh][0].start()
        downs[hh][0].start()
    for hh in range(2):
        process(0, hh)
    for s in range(3):
        for hh in range(2):
            ups[hh][s].wait_recv()
            ups[hh][s + 1].start()
            downs[hh][s].wait_recv()
            downs[hh][s + 1].start()
            process(1 + 2 * s, hh)
            process(2 + 2 * s, hh)
    for hh in range(2):
        ups[hh][3].wait_recv()
        downs[hh][3].wait_recv()
        process(7, hh)
    for local, sends in started:
        local.wait()
        for cp in sends:
            cp.wait()
    for hh in range(2):
        for cp in ups[hh] + downs[hh]:
            cp.wait_send()


def exchange_out(code, own):
    n, _, rows, cols = own.shape
    blocks = pltpu.VMEM((n, rows, cols), own.dtype)
    dma = pltpu.SemaphoreType.DMA
    return pl.pallas_call(
        out_kernel,
        out_shape=jax.ShapeDtypeStruct((64, 2, rows, cols), own.dtype),
        in_specs=[pl.BlockSpec(memory_space=pltpu.SMEM), pl.BlockSpec(memory_space=pltpu.VMEM)],
        out_specs=pl.BlockSpec(memory_space=pl.ANY),
        scratch_shapes=[[blocks] * 2] * 7 + [
            pltpu.VMEM((8, 2, 8, rows, cols), own.dtype),
            dma((8, 2)), dma((8, 2)), dma((8, 2, 8)), dma((64, 2)), dma((8, 2)),
        ],
        compiler_params=pltpu.CompilerParams(
            collective_id=0, has_side_effects=True, vmem_limit_bytes=VMEM_LIMIT),
        cost_estimate=pl.CostEstimate(flops=0, bytes_accessed=250_000_000, transcendentals=0),
        name="exchange_out",
    )(code, own)


def back_kernel(code_ref, own, grad, tokens, weight, out, token_grad, wout,
                zp0, zp1, zm0, zm1, st_up, st_dn, zp2, zm2, z4, sbuf,
                gathered, share, crecv, s_own, s_up, s_dn, s_far, y_a, y_b, y_up, y_dn,
                w_up1, w_up, w_dn1, w_dn,
                zs, zr, ysend, yrecv, ls, xs, xr, cs, cr, ws, wr, us, ur):
    p = Place()
    up, down = p.dev(0, 1), p.dev(0, -1)
    yup, ydn = p.dev(1), p.dev(-1)
    far = [p.dev(dx=1), p.dev(dx=-1), p.dev(dx=2)]
    greet([up, down] + plane_partners(p) + far)
    first, last = pl.ds(8, 4), pl.ds(8, 4)
    ups, downs = [], []
    for hh in range(2):
        ups.append([remote(own.at[:, hh], zp0[hh], zs.at[0, hh], zr.at[0, hh], up),
                    remote(zp0[hh], zp1[hh], zs.at[1, hh], zr.at[1, hh], up),
                    remote(st_up.at[hh], zp2.at[hh], zs.at[2, hh], zr.at[2, hh], up),
                    remote(zp2.at[hh, first], z4.at[hh, pl.ds(0, 4)], zs.at[3, hh], zr.at[3, hh], up)])
        downs.append([remote(own.at[:, hh], zm0[hh], zs.at[4, hh], zr.at[4, hh], down),
                      remote(zm0[hh], zm1[hh], zs.at[5, hh], zr.at[5, hh], down),
                      remote(st_dn.at[hh], zm2.at[hh], zs.at[6, hh], zr.at[6, hh], down),
                      remote(zm2.at[hh, last], z4.at[hh, pl.ds(4, 4)], zs.at[7, hh], zr.at[7, hh], down)])
    sets = [None, zp0, zm0, zp1, zm1]
    started = []

    def pick(origin, target):
        return (code_ref[origin * 64 + target] // 8) % 16

    def process(k, hh):
        origin = p.dp(0, Z_OFF[k], 0)
        for i, (dy, dc) in enumerate(J_OFF):
            r = pick(origin, p.dp(dy, 0, dc))
            sbuf[k, hh, i] = own[r, hh] if k == 0 else sets[k][hh][r]
        started.append(plane_send(p, out, k, hh, lambda i: sbuf.at[k, hh, i], ysend, yrecv, ls))

    def forward(k, hh, buf):
        started.append(plane_send(p, out, k, hh, lambda i: buf.at[hh, i], ysend, yrecv, ls))

    def stage(hh, held, staged, way, part):
        origin = p.dp(0, -2 * way, 0)
        for i, (dy, dc) in enumerate(J_OFF):
            staged[hh, i] = held[hh][pick(origin, p.dp(dy, way, dc))]
        for i in range(4):
            dy, dc = J_OFF[part + i]
            staged[hh, 8 + i] = held[hh][pick(origin, p.dp(dy, 2 * way, dc))]

    gathers = [remote(grad, gathered.at[p.x], xs.at[i], xr.at[i], d) for i, d in enumerate(far)]
    for cp in gathers:
        cp.start()
    for hh in range(2):
        ups[hh][0].start()
        downs[hh][0].start()
    gathered[p.x] = grad[...]
    for hh in range(2):
        process(0, hh)

    def hop1(hh):
        ups[hh][0].wait_recv()
        ups[hh][1].start()
        downs[hh][0].wait_recv()
        downs[hh][1].start()
        process(1, hh)
        process(2, hh)

    hop1(0)
    for cp in gathers:
        cp.wait_recv()

    tn = (((0,), (0,)), ((), ()))
    nt = (((1,), (1,)), ((), ()))
    pairs = []
    for n, dy in enumerate((2, 1, -1, 0)):
        yy = (p.y + dy + NY) % NY

        @pl.loop(0, 2)
        def _(r, yy=yy, n=n):
            cols = pl.ds(pl.multiple_of(r * 256, 256), 256)
            part = lax.dot_general(gathered[yy, :, cols], tokens[...], tn, preferred_element_type=jnp.float32)
            share[n, pl.ds(r * 4, 4)] = part.reshape(4, 2, 32, part.shape[1])

        cp = remote(share.at[n, :, 1 - p.c], crecv.at[n], cs.at[n], cr.at[n], p.dev(0, 0, 1))
        cp.start()
        pairs.append(cp)

    hop1(1)

    sums = [s_far, s_up, s_dn, s_own]
    for n in range(4):
        pairs[n].wait_recv()

        @pl.loop(0, NZ)
        def _(i, n=n):
            sums[n][i] = share[n, i, p.c] + crecv[n, i]

        if n == 0:
            far_up = remote(s_far.at[pl.ds(0, 4)], y_a, ws.at[0], wr.at[0], yup)
            far_dn = remote(s_far.at[pl.ds(4, 4)], y_b, ws.at[1], wr.at[1], ydn)
            far_up.start()
            far_dn.start()

    @pl.loop(0, 4)
    def _(i):
        rows = pl.ds(pl.multiple_of(i * 128, 128), 128)
        total = jnp.zeros((128, weight.shape[0]), jnp.float32)
        for a in range(4):
            total += lax.dot_general(gathered[a, rows, :], weight[:, a * 512:(a + 1) * 512], nt,
                                     preferred_element_type=jnp.float32)
        token_grad[rows, :] = total.astype(token_grad.dtype)

    far_up.wait_recv()

    @pl.loop(0, 4)
    def _(i):
        s_up[i] += y_a[i]

    near_up = remote(s_up, y_up, ws.at[2], wr.at[2], yup)
    near_up.start()
    far_dn.wait_recv()

    @pl.loop(0, 4)
    def _(i):
        s_dn[4 + i] += y_b[i]

    near_dn = remote(s_dn, y_dn, ws.at[3], wr.at[3], ydn)
    near_dn.start()

    def hop2(hh):
        ups[hh][1].wait_recv()
        stage(hh, zp1, st_up, 1, 0)
        ups[hh][2].start()
        downs[hh][1].wait_recv()
        stage(hh, zm1, st_dn, -1, 4)
        downs[hh][2].start()
        process(3, hh)
        process(4, hh)

    def hop3(hh):
        ups[hh][2].wait_recv()
        ups[hh][3].start()
        downs[hh][2].wait_recv()
        downs[hh][3].start()
        forward(5, hh, zp2)
        forward(6, hh, zm2)

    def hop4(hh):
        ups[hh][3].wait_recv()
        downs[hh][3].wait_recv()
        forward(7, hh, z4)

    hop2(0)
    hop2(1)
    near_up.wait_recv()
    near_dn.wait_recv()

    @pl.loop(0, NZ)
    def _(i):
        s_own[i] += y_up[i] + y_dn[i]

    def at(dz):
        return (p.z + dz + NZ) % NZ

    chain_up = [remote(s_own.at[at(4), pl.ds(0, 16)], w_up1, us.at[0], ur.at[0], up)]
    chain_dn = [remote(s_own.at[at(4), pl.ds(16, 16)], w_dn1, us.at[4], ur.at[4], down)]
    for i, dz in enumerate((3, 2, 1)):
        chain_up.append(remote(s_own.at[at(dz)], w_up.at[i], us.at[1 + i], ur.at[1 + i], up))
        chain_dn.append(remote(s_own.at[at(-dz)], w_dn.at[i], us.at[5 + i], ur.at[5 + i], down))

    def ring(step):
        if step == 1:
            chain_up[0].wait_recv()
            s_own[at(3), pl.ds(0, 16)] += w_up1[...]
            chain_dn[0].wait_recv()
            s_own[at(-3), pl.ds(16, 16)] += w_dn1[...]
        elif step > 1:
            chain_up[step - 1].wait_recv()
            s_own[at(4 - step)] += w_up[step - 2]
            chain_dn[step - 1].wait_recv()
            s_own[at(step - 4)] += w_dn[step - 2]
        if step < 4:
            chain_up[step].start()
            chain_dn[step].start()

    ring(0)
    hop3(0)
    ring(1)
    hop3(1)
    ring(2)
    hop4(0)
    ring(3)
    hop4(1)
    chain_up[3].wait_recv()
    chain_dn[3].wait_recv()
    wout[...] = s_own[p.z] + w_up[2] + w_dn[2]

    for local, sends in started:
        local.wait()
        for cp in sends:
            cp.wait()
    for hh in range(2):
        for cp in ups[hh] + downs[hh]:
            cp.wait_send()
    for cp in gathers + pairs + [far_up, far_dn, near_up, near_dn] + chain_up + chain_dn:
        cp.wait_send()


def exchange_back(code, own, grad, tokens, weight):
    n, _, rows, cols = own.shape
    toks, feats = tokens.shape
    low, full = jnp.bfloat16, jnp.float32
    blocks = lambda count: pltpu.VMEM((2, count, rows, cols), low)
    lump = lambda *lead: pltpu.VMEM(lead + (32, feats), full)
    dma = pltpu.SemaphoreType.DMA
    vmem = pl.BlockSpec(memory_space=pltpu.VMEM)
    return pl.pallas_call(
        back_kernel,
        out_shape=[
            jax.ShapeDtypeStruct((64, 2, rows, cols), low),
            jax.ShapeDtypeStruct((toks, feats), low),
            jax.ShapeDtypeStruct((32, feats), full),
        ],
        in_specs=[pl.BlockSpec(memory_space=pltpu.SMEM), vmem, vmem, vmem, vmem],
        out_specs=[pl.BlockSpec(memory_space=pl.ANY), vmem, vmem],
        scratch_shapes=[[pltpu.VMEM((n, rows, cols), low)] * 2] * 4 + [blocks(12)] * 4 + [
            blocks(8),
            pltpu.VMEM((5, 2, 8, rows, cols), low),
            pltpu.VMEM((4, toks, grad.shape[1]), low),
            lump(4, NZ, 2), lump(4, NZ), lump(NZ), lump(NZ), lump(NZ), lump(NZ),
            lump(4), lump(4), lump(NZ), lump(NZ),
            pltpu.VMEM((16, feats), full), lump(3), pltpu.VMEM((16, feats), full), lump(3),
            dma((8, 2)), dma((8, 2)), dma((8, 2, 8)), dma((64, 2)), dma((8, 2)),
            dma((3,)), dma((3,)), dma((4,)), dma((4,)), dma((4,)), dma((4,)), dma((8,)), dma((8,)),
        ],
        compiler_params=pltpu.CompilerParams(
            collective_id=1, has_side_effects=True, vmem_limit_bytes=VMEM_LIMIT),
        cost_estimate=pl.CostEstimate(flops=0, bytes_accessed=250_000_000, transcendentals=0),
        name="exchange_back",
    )(code, own, grad, tokens, weight)


def attention_kernel(pos_ref, q_ref, g_ref, kv0_ref, kv1_ref, att_ref, qg_ref, bg_ref):
    heads = kv0_ref.shape[1]
    width = q_ref.shape[1] // heads
    near = kv0_ref.shape[2]
    root = 1.0 / math.sqrt(width)
    zero = jnp.zeros((SPAN, width), jnp.bfloat16)
    nt = (((1,), (1,)), ((), ()))
    nn = (((1,), (0,)), ((), ()))
    tn = (((0,), (0,)), ((), ()))

    def dot(a, b, dims):
        return lax.dot_general(a, b, dims, preferred_element_type=jnp.float32)

    for h in range(heads):
        cols = slice(h * width, (h + 1) * width)
        q, g = q_ref[:, cols], g_ref[:, cols]
        kv = jnp.concatenate([kv0_ref[0, h], kv1_ref[0, h]], axis=0)
        both = jnp.concatenate(
            [jnp.concatenate([q, zero], axis=1), jnp.concatenate([zero, g], axis=1)], axis=0)
        raw = dot(both, kv, nt)
        score = raw[:SPAN] * root
        prob_grad = raw[SPAN:]
        weights = jnp.exp(score - jnp.max(score, axis=-1, keepdims=True))
        probs = weights / jnp.sum(weights, axis=-1, keepdims=True)
        low = probs.astype(jnp.bfloat16)
        term = jnp.sum(probs * prob_grad, axis=-1, keepdims=True)
        sg = (probs * (prob_grad - term)).astype(jnp.bfloat16)
        applied = dot(jnp.concatenate([low, sg], axis=0), kv, nn)
        att_ref[:, cols] = applied[:SPAN, width:].astype(jnp.bfloat16)
        qg_ref[:, cols] = (applied[SPAN:, :width] * root).astype(jnp.bfloat16)
        back = dot(jnp.concatenate([sg, low], axis=0), both, tn)
        lane = lax.broadcasted_iota(jnp.int32, back.shape, 1)
        back = (back * jnp.where(lane < width, root, 1.0)).astype(jnp.bfloat16)
        bg_ref[0, h] = back[:near]
        bg_ref[1, h] = back[near:]


def attention(pos, queries, grads, blocks):
    rows, cols = queries.shape
    spans = rows // SPAN
    _, heads, near, pair = blocks.shape
    kv = lambda n: pl.BlockSpec((1, heads, near, pair), lambda i, pos: (pos[2 * i + n], 0, 0, 0))
    flat = pl.BlockSpec((SPAN, cols), lambda i, pos: (i, 0))
    return pl.pallas_call(
        attention_kernel,
        grid_spec=pltpu.PrefetchScalarGridSpec(
            num_scalar_prefetch=1,
            grid=(spans,),
            in_specs=[flat, flat, kv(0), kv(1)],
            out_specs=[flat, flat, pl.BlockSpec((2, heads, near, pair), lambda i, pos: (i, 0, 0, 0))],
        ),
        out_shape=[
            jax.ShapeDtypeStruct((rows, cols), jnp.bfloat16),
            jax.ShapeDtypeStruct((rows, cols), jnp.bfloat16),
            jax.ShapeDtypeStruct((2 * spans, heads, near, pair), jnp.bfloat16),
        ],
        compiler_params=pltpu.CompilerParams(vmem_limit_bytes=VMEM_LIMIT),
        name="attention",
    )(pos, queries, grads, blocks, blocks)


def gather_sum_kernel(code_ref, blk_ref, out_ref, acc):
    h = pl.program_id(0)
    acc[...] = jnp.zeros_like(acc)

    def body(i, carry):
        code = code_ref[i]

        @pl.when(code >= 128)
        def _():
            e = code % 8
            acc[e] += blk_ref[i, 0].astype(jnp.float32)

        return carry

    lax.fori_loop(0, 64, body, 0)
    out_ref[0] = acc[...]


def gather_sum(codes, blocks):
    _, heads, near, pair = blocks.shape
    return pl.pallas_call(
        gather_sum_kernel,
        grid=(heads,),
        in_specs=[
            pl.BlockSpec(memory_space=pltpu.SMEM),
            pl.BlockSpec((64, 1, near, pair), lambda h: (0, h, 0, 0)),
        ],
        out_specs=pl.BlockSpec((1, 8, near, pair), lambda h: (h, 0, 0, 0)),
        out_shape=jax.ShapeDtypeStruct((heads, 8, near, pair), jnp.float32),
        scratch_shapes=[pltpu.VMEM((8, near, pair), jnp.float32)],
        compiler_params=pltpu.CompilerParams(vmem_limit_bytes=VMEM_LIMIT),
        name="gather_sum",
    )(codes, blocks)


def slot_devices(me):
    y, z, c = me // (2 * NZ), (me // 2) % NZ, me % 2
    ys = jnp.array([j[0] for j in J_OFF], jnp.int32)[:, None]
    cs = jnp.array([j[1] for j in J_OFF], jnp.int32)[:, None]
    zs = jnp.array(Z_OFF, jnp.int32)[None, :]
    return dp_of((y + ys + NY) % NY, (z + zs + NZ) % NZ, (c + cs) % 2).reshape(-1)


def on_device(tokens, query_weight, neighbour_store, neighbours, attended_grad):
    entries_here, near, heads, pair = neighbour_store.shape
    me = lax.axis_index("dp")
    fields = lax.psum_scatter(
        lax.dot_general(
            query_weight, tokens, (((0,), (1,)), ((), ())), preferred_element_type=jnp.float32
        ),
        "fsdp",
        scatter_dimension=0,
        tiled=True,
    )
    queries = fields.T.astype(jnp.bfloat16)

    refs = neighbours.reshape(64, -1)
    order = jnp.arange(refs.shape[1], dtype=jnp.int32)[None, :]
    word = 128 + 8 * order + refs % entries_here
    shard = jnp.arange(64, dtype=jnp.int32)
    table = jnp.max(
        jnp.where((refs // entries_here)[:, :, None] == shard, word[:, :, None], 0), axis=1)
    code = table.reshape(-1)

    slots = slot_devices(me)
    mine = lax.dynamic_index_in_dim(refs, me, 0, keepdims=False) // entries_here
    pos = jnp.sum(
        jnp.where(mine[:, None] == slots[None, :], jnp.arange(64, dtype=jnp.int32)[None, :], 0), axis=1)

    store = neighbour_store.transpose(0, 2, 1, 3).reshape(entries_here, 2, heads * near // 2, pair)
    got = exchange_out(code, store).reshape(64, heads, near, pair)
    attended, query_grad, block_grad = attention(pos, queries, attended_grad, got)
    halves = block_grad.reshape(-1, 2, heads * near // 2, pair)
    back, token_grad, weight_share = exchange_back(code, halves, query_grad, tokens, query_weight)
    weight_grad = weight_share.T
    column = jnp.take(table, slots, axis=0)
    column = lax.dynamic_index_in_dim(column, me, 1, keepdims=False)
    summed = gather_sum(column, back.reshape(64, heads, near, pair))
    store_grad = summed.transpose(1, 2, 0, 3)
    return (attended, token_grad, weight_grad, store_grad)


def solution(mesh):
    return jax.shard_map(
        on_device,
        mesh=mesh,
        in_specs=(
            P("dp", "fsdp"),
            P("fsdp", None),
            P("dp", None, "fsdp", None),
            P(),
            P("dp", "fsdp"),
        ),
        out_specs=(P("dp", "fsdp"), P("dp", "fsdp"), P("fsdp", "dp"), P("dp", None, "fsdp", None)),
        check_vma=False,
    )
```

```python
import functools
import math

import jax
import jax.numpy as jnp
from jax import lax
from jax.experimental import pallas as pl
from jax.experimental.pallas import tpu as pltpu
from jax.sharding import PartitionSpec as P

SPAN = 64
NY, NZ = 4, 8
MESH = pl.DeviceIdType.MESH
Z_OFF = (0, -1, 1, -2, 2, -3, 3, 4)
J_OFF = ((0, 0), (0, 1), (-1, 0), (-1, 1), (1, 0), (1, 1), (2, 0), (2, 1))
VMEM_LIMIT = 60 * 1024 * 1024


def dp_of(y, z, c):
    return (y * NZ + z) * 2 + c


class Place:
    def __init__(self):
        me = lax.axis_index("dp")
        self.x = lax.axis_index("fsdp")
        self.y, self.z, self.c = me // (2 * NZ), (me // 2) % NZ, me % 2

    def dp(self, dy, dz, dc):
        return dp_of((self.y + dy + NY) % NY, (self.z + dz + NZ) % NZ, (self.c + dc) % 2)

    def dev(self, dy=0, dz=0, dc=0, dx=0):
        return (self.dp(dy, dz, dc), (self.x + dx + 4) % 4)


def greet(devices):
    barrier = pltpu.get_barrier_semaphore()
    for d in devices:
        pl.semaphore_signal(barrier, inc=1, device_id=d, device_id_type=MESH)
    pl.semaphore_wait(barrier, len(devices))


def remote(src, dst, ssem, rsem, d):
    return pltpu.make_async_remote_copy(
        src_ref=src, dst_ref=dst, send_sem=ssem, recv_sem=rsem, device_id=d, device_id_type=MESH)


def plane_partners(p):
    return [p.dev(dy, 0, dc) for dy, dc in J_OFF[1:]]


def plane_send(p, out, k, hh, blocks, ysend, yrecv, ls):
    local = pltpu.make_async_copy(blocks(0), out.at[k, hh], ls.at[k, hh])
    local.start()
    sends = []
    for i, j in ((1, 1), (6, 6), (7, 7), (4, 2), (5, 3), (2, 4), (3, 5)):
        dy, dc = J_OFF[i]
        cp = remote(blocks(i), out.at[j * 8 + k, hh], ysend.at[k, hh, i], yrecv.at[j * 8 + k, hh],
                    p.dev(dy, 0, dc))
        cp.start()
        sends.append(cp)
    return local, sends


def out_kernel(code_ref, own, tokens, weight, out, queries, zp0, zp1, zp2, zm0, zm1, zm2, z4, sbuf,
               toks, wgt, part, q_a, q_b, q_up, q_dn,
               zs, zr, ysend, yrecv, ls, fetch, xs, xr):
    p = Place()
    half = own.shape[0] // 2
    fetches = [pltpu.make_async_copy(tokens, toks, fetch.at[0]),
               pltpu.make_async_copy(weight, wgt, fetch.at[1])]
    for cp in fetches:
        cp.start()
    up, down = p.dev(0, 1), p.dev(0, -1)
    xup, xdn = p.dev(dx=1), p.dev(dx=-1)
    greet([up, down, xup, xdn] + plane_partners(p))
    zp, zm = [zp0, zp1, zp2], [zm0, zm1, zm2]
    lo, hi = pl.ds(0, half), pl.ds(half, half)
    ups, downs = [], []
    for hh in range(2):
        ups.append([remote(own.at[:, hh], zp0[hh], zs.at[0, hh], zr.at[0, hh], up),
                    remote(zp0[hh], zp1[hh], zs.at[1, hh], zr.at[1, hh], up),
                    remote(zp1[hh], zp2[hh], zs.at[2, hh], zr.at[2, hh], up),
                    remote(zp2[hh].at[lo], z4[hh].at[lo], zs.at[3, hh], zr.at[3, hh], up)])
        downs.append([remote(own.at[:, hh], zm0[hh], zs.at[4, hh], zr.at[4, hh], down),
                      remote(zm0[hh], zm1[hh], zs.at[5, hh], zr.at[5, hh], down),
                      remote(zm1[hh], zm2[hh], zs.at[6, hh], zr.at[6, hh], down),
                      remote(zm2[hh].at[hi], z4[hh].at[hi], zs.at[7, hh], zr.at[7, hh], down)])
    sets = [None, zp0, zm0, zp1, zm1, zp2, zm2, z4]
    started = []

    def process(k, hh):
        origin = p.dp(0, Z_OFF[k], 0)
        for i, (dy, dc) in enumerate(J_OFF):
            pick = code_ref[p.dp(dy, 0, dc) * 64 + origin] % 8
            sbuf[k, hh, i] = own[pick, hh] if k == 0 else sets[k][hh][pick]
        started.append(plane_send(p, out, k, hh, lambda i: sbuf.at[k, hh, i], ysend, yrecv, ls))

    for hh in range(2):
        ups[hh][0].start()
        downs[hh][0].start()
    for hh in range(2):
        process(0, hh)

    for cp in fetches:
        cp.wait()
    rows, width = queries.shape
    top, bottom = pl.ds(0, rows // 2), pl.ds(rows // 2, rows // 2)
    for n, dx in enumerate((2, 1, -1, 0)):
        cols = pl.ds(pl.multiple_of((p.x + dx + 4) % 4 * width, width), width)

        @pl.loop(0, 4)
        def _(r, n=n, cols=cols):
            some = pl.ds(pl.multiple_of(r * (rows // 4), rows // 4), rows // 4)
            part[n][some, :] = jnp.dot(toks[some, :], wgt[:, cols], preferred_element_type=jnp.float32)

        if n == 0:
            far_up = remote(part[0].at[top], q_a, xs.at[0], xr.at[0], xup)
            far_dn = remote(part[0].at[bottom], q_b, xs.at[1], xr.at[1], xdn)
            far_up.start()
            far_dn.start()

    near_up = remote(part[1], q_up, xs.at[2], xr.at[2], xup)
    near_dn = remote(part[2], q_dn, xs.at[3], xr.at[3], xdn)
    for s in range(3):
        for hh in range(2):
            ups[hh][s].wait_recv()
            ups[hh][s + 1].start()
            downs[hh][s].wait_recv()
            downs[hh][s + 1].start()
            process(1 + 2 * s, hh)
            process(2 + 2 * s, hh)
        if s == 0:
            far_up.wait_recv()
            part[1][top, :] += q_a[...]
            near_up.start()
            far_dn.wait_recv()
            part[2][bottom, :] += q_b[...]
            near_dn.start()
    near_up.wait_recv()
    near_dn.wait_recv()
    queries[...] = (part[3][...] + q_up[...] + q_dn[...]).astype(queries.dtype)
    for hh in range(2):
        ups[hh][3].wait_recv()
        downs[hh][3].wait_recv()
        process(7, hh)
    for local, sends in started:
        local.wait()
        for cp in sends:
            cp.wait()
    for hh in range(2):
        for cp in ups[hh] + downs[hh]:
            cp.wait_send()
    for cp in (far_up, far_dn, near_up, near_dn):
        cp.wait_send()


def exchange_out(code, own, tokens, weight):
    n, _, rows, cols = own.shape
    blocks = pltpu.VMEM((n, rows, cols), own.dtype)
    dma = pltpu.SemaphoreType.DMA
    hbm = pl.BlockSpec(memory_space=pl.ANY)
    count, width = tokens.shape[0], weight.shape[1] // 4
    total = pltpu.VMEM((count, width), jnp.float32)
    part = pltpu.VMEM((count // 2, width), jnp.float32)
    return pl.pallas_call(
        out_kernel,
        out_shape=[
            jax.ShapeDtypeStruct((64, 2, rows, cols), own.dtype),
            jax.ShapeDtypeStruct((count, width), own.dtype),
        ],
        in_specs=[pl.BlockSpec(memory_space=pltpu.SMEM), pl.BlockSpec(memory_space=pltpu.VMEM), hbm, hbm],
        out_specs=[hbm, pl.BlockSpec(memory_space=pltpu.VMEM)],
        scratch_shapes=[[blocks] * 2] * 7 + [
            pltpu.VMEM((8, 2, 8, rows, cols), own.dtype),
            pltpu.VMEM(tokens.shape, tokens.dtype), pltpu.VMEM(weight.shape, weight.dtype),
            [total] * 4, part, part, total, total,
            dma((8, 2)), dma((8, 2)), dma((8, 2, 8)), dma((64, 2)), dma((8, 2)),
            dma((2,)), dma((4,)), dma((4,)),
        ],
        compiler_params=pltpu.CompilerParams(
            collective_id=0, has_side_effects=True, vmem_limit_bytes=VMEM_LIMIT),
        cost_estimate=pl.CostEstimate(flops=0, bytes_accessed=250_000_000, transcendentals=0),
        name="exchange_out",
    )(code, own, tokens, weight)


def back_kernel(code_ref, own, grad, tokens_far, weight_far, out, token_grad, wout,
                zp0, zp1, zm0, zm1, st_up, st_dn, zp2, zm2, z4, sbuf,
                gathered, share, crecv, s_own, s_up, s_dn, s_far, y_a, y_b, y_up, y_dn,
                w_up1, w_up, w_dn1, w_dn, tokens, weight,
                zs, zr, ysend, yrecv, ls, xs, xr, cs, cr, ws, wr, us, ur, fetch):
    p = Place()
    fetches = [pltpu.make_async_copy(tokens_far, tokens, fetch.at[0]),
               pltpu.make_async_copy(weight_far, weight, fetch.at[1])]
    for cp in fetches:
        cp.start()
    up, down = p.dev(0, 1), p.dev(0, -1)
    yup, ydn = p.dev(1), p.dev(-1)
    far = [p.dev(dx=1), p.dev(dx=-1), p.dev(dx=2)]
    greet([up, down] + plane_partners(p) + far)
    first, last = pl.ds(8, 4), pl.ds(8, 4)
    ups, downs = [], []
    for hh in range(2):
        ups.append([remote(own.at[:, hh], zp0[hh], zs.at[0, hh], zr.at[0, hh], up),
                    remote(zp0[hh], zp1[hh], zs.at[1, hh], zr.at[1, hh], up),
                    remote(st_up.at[hh], zp2.at[hh], zs.at[2, hh], zr.at[2, hh], up),
                    remote(zp2.at[hh, first], z4.at[hh, pl.ds(0, 4)], zs.at[3, hh], zr.at[3, hh], up)])
        downs.append([remote(own.at[:, hh], zm0[hh], zs.at[4, hh], zr.at[4, hh], down),
                      remote(zm0[hh], zm1[hh], zs.at[5, hh], zr.at[5, hh], down),
                      remote(st_dn.at[hh], zm2.at[hh], zs.at[6, hh], zr.at[6, hh], down),
                      remote(zm2.at[hh, last], z4.at[hh, pl.ds(4, 4)], zs.at[7, hh], zr.at[7, hh], down)])
    sets = [None, zp0, zm0, zp1, zm1]
    started = []

    def pick(origin, target):
        return (code_ref[origin * 64 + target] // 8) % 16

    def process(k, hh):
        origin = p.dp(0, Z_OFF[k], 0)
        for i, (dy, dc) in enumerate(J_OFF):
            r = pick(origin, p.dp(dy, 0, dc))
            sbuf[k, hh, i] = own[r, hh] if k == 0 else sets[k][hh][r]
        started.append(plane_send(p, out, k, hh, lambda i: sbuf.at[k, hh, i], ysend, yrecv, ls))

    def forward(k, hh, buf):
        started.append(plane_send(p, out, k, hh, lambda i: buf.at[hh, i], ysend, yrecv, ls))

    def stage(hh, held, staged, way, part):
        origin = p.dp(0, -2 * way, 0)
        for i, (dy, dc) in enumerate(J_OFF):
            staged[hh, i] = held[hh][pick(origin, p.dp(dy, way, dc))]
        for i in range(4):
            dy, dc = J_OFF[part + i]
            staged[hh, 8 + i] = held[hh][pick(origin, p.dp(dy, 2 * way, dc))]

    gathers = [remote(grad, gathered.at[p.x], xs.at[i], xr.at[i], d) for i, d in enumerate(far)]
    for cp in gathers:
        cp.start()
    for hh in range(2):
        ups[hh][0].start()
        downs[hh][0].start()
    gathered[p.x] = grad[...]
    for hh in range(2):
        process(0, hh)

    def hop1(hh):
        ups[hh][0].wait_recv()
        ups[hh][1].start()
        downs[hh][0].wait_recv()
        downs[hh][1].start()
        process(1, hh)
        process(2, hh)

    hop1(0)
    for cp in gathers:
        cp.wait_recv()
    for cp in fetches:
        cp.wait()

    tn = (((0,), (0,)), ((), ()))
    nt = (((1,), (1,)), ((), ()))
    pairs = []
    for n, dy in enumerate((2, 1, -1, 0)):
        yy = (p.y + dy + NY) % NY

        @pl.loop(0, 2)
        def _(r, yy=yy, n=n):
            cols = pl.ds(pl.multiple_of(r * 256, 256), 256)
            part = lax.dot_general(gathered[yy, :, cols], tokens[...], tn, preferred_element_type=jnp.float32)
            share[n, pl.ds(r * 4, 4)] = part.reshape(4, 2, 32, part.shape[1])

        cp = remote(share.at[n, :, 1 - p.c], crecv.at[n], cs.at[n], cr.at[n], p.dev(0, 0, 1))
        cp.start()
        pairs.append(cp)

    hop1(1)

    sums = [s_far, s_up, s_dn, s_own]
    for n in range(4):
        pairs[n].wait_recv()

        @pl.loop(0, NZ)
        def _(i, n=n):
            sums[n][i] = share[n, i, p.c] + crecv[n, i]

        if n == 0:
            far_up = remote(s_far.at[pl.ds(0, 4)], y_a, ws.at[0], wr.at[0], yup)
            far_dn = remote(s_far.at[pl.ds(4, 4)], y_b, ws.at[1], wr.at[1], ydn)
            far_up.start()
            far_dn.start()

    @pl.loop(0, 4)
    def _(i):
        rows = pl.ds(pl.multiple_of(i * 128, 128), 128)
        total = jnp.zeros((128, weight.shape[0]), jnp.float32)
        for a in range(4):
            total += lax.dot_general(gathered[a, rows, :], weight[:, a * 512:(a + 1) * 512], nt,
                                     preferred_element_type=jnp.float32)
        token_grad[rows, :] = total.astype(token_grad.dtype)

    far_up.wait_recv()

    @pl.loop(0, 4)
    def _(i):
        s_up[i] += y_a[i]

    near_up = remote(s_up, y_up, ws.at[2], wr.at[2], yup)
    near_up.start()
    far_dn.wait_recv()

    @pl.loop(0, 4)
    def _(i):
        s_dn[4 + i] += y_b[i]

    near_dn = remote(s_dn, y_dn, ws.at[3], wr.at[3], ydn)
    near_dn.start()

    def hop2(hh):
        ups[hh][1].wait_recv()
        stage(hh, zp1, st_up, 1, 0)
        ups[hh][2].start()
        downs[hh][1].wait_recv()
        stage(hh, zm1, st_dn, -1, 4)
        downs[hh][2].start()
        process(3, hh)
        process(4, hh)

    def hop3(hh):
        ups[hh][2].wait_recv()
        ups[hh][3].start()
        downs[hh][2].wait_recv()
        downs[hh][3].start()
        forward(5, hh, zp2)
        forward(6, hh, zm2)

    def hop4(hh):
        ups[hh][3].wait_recv()
        downs[hh][3].wait_recv()
        forward(7, hh, z4)

    hop2(0)
    hop2(1)
    near_up.wait_recv()
    near_dn.wait_recv()

    @pl.loop(0, NZ)
    def _(i):
        s_own[i] += y_up[i] + y_dn[i]

    def at(dz):
        return (p.z + dz + NZ) % NZ

    chain_up = [remote(s_own.at[at(4), pl.ds(0, 16)], w_up1, us.at[0], ur.at[0], up)]
    chain_dn = [remote(s_own.at[at(4), pl.ds(16, 16)], w_dn1, us.at[4], ur.at[4], down)]
    for i, dz in enumerate((3, 2, 1)):
        chain_up.append(remote(s_own.at[at(dz)], w_up.at[i], us.at[1 + i], ur.at[1 + i], up))
        chain_dn.append(remote(s_own.at[at(-dz)], w_dn.at[i], us.at[5 + i], ur.at[5 + i], down))

    def ring(step):
        if step == 1:
            chain_up[0].wait_recv()
            s_own[at(3), pl.ds(0, 16)] += w_up1[...]
            chain_dn[0].wait_recv()
            s_own[at(-3), pl.ds(16, 16)] += w_dn1[...]
        elif step > 1:
            chain_up[step - 1].wait_recv()
            s_own[at(4 - step)] += w_up[step - 2]
            chain_dn[step - 1].wait_recv()
            s_own[at(step - 4)] += w_dn[step - 2]
        if step < 4:
            chain_up[step].start()
            chain_dn[step].start()

    ring(0)
    hop3(0)
    ring(1)
    hop3(1)
    ring(2)
    hop4(0)
    ring(3)
    hop4(1)
    chain_up[3].wait_recv()
    chain_dn[3].wait_recv()
    wout[...] = s_own[p.z] + w_up[2] + w_dn[2]

    for local, sends in started:
        local.wait()
        for cp in sends:
            cp.wait()
    for hh in range(2):
        for cp in ups[hh] + downs[hh]:
            cp.wait_send()
    for cp in gathers + pairs + [far_up, far_dn, near_up, near_dn] + chain_up + chain_dn:
        cp.wait_send()


def exchange_back(code, own, grad, tokens, weight):
    n, _, rows, cols = own.shape
    toks, feats = tokens.shape
    low, full = jnp.bfloat16, jnp.float32
    blocks = lambda count: pltpu.VMEM((2, count, rows, cols), low)
    lump = lambda *lead: pltpu.VMEM(lead + (32, feats), full)
    dma = pltpu.SemaphoreType.DMA
    vmem = pl.BlockSpec(memory_space=pltpu.VMEM)
    hbm = pl.BlockSpec(memory_space=pl.ANY)
    return pl.pallas_call(
        back_kernel,
        out_shape=[
            jax.ShapeDtypeStruct((64, 2, rows, cols), low),
            jax.ShapeDtypeStruct((toks, feats), low),
            jax.ShapeDtypeStruct((32, feats), full),
        ],
        in_specs=[pl.BlockSpec(memory_space=pltpu.SMEM), vmem, vmem, hbm, hbm],
        out_specs=[pl.BlockSpec(memory_space=pl.ANY), vmem, vmem],
        scratch_shapes=[[pltpu.VMEM((n, rows, cols), low)] * 2] * 4 + [blocks(12)] * 4 + [
            blocks(8),
            pltpu.VMEM((5, 2, 8, rows, cols), low),
            pltpu.VMEM((4, toks, grad.shape[1]), low),
            lump(4, NZ, 2), lump(4, NZ), lump(NZ), lump(NZ), lump(NZ), lump(NZ),
            lump(4), lump(4), lump(NZ), lump(NZ),
            pltpu.VMEM((16, feats), full), lump(3), pltpu.VMEM((16, feats), full), lump(3),
            pltpu.VMEM(tokens.shape, low), pltpu.VMEM(weight.shape, low),
            dma((8, 2)), dma((8, 2)), dma((8, 2, 8)), dma((64, 2)), dma((8, 2)),
            dma((3,)), dma((3,)), dma((4,)), dma((4,)), dma((4,)), dma((4,)), dma((8,)), dma((8,)), dma((2,)),
        ],
        compiler_params=pltpu.CompilerParams(
            collective_id=1, has_side_effects=True, vmem_limit_bytes=VMEM_LIMIT),
        cost_estimate=pl.CostEstimate(flops=0, bytes_accessed=250_000_000, transcendentals=0),
        name="exchange_back",
    )(code, own, grad, tokens, weight)


def attention_kernel(pos_ref, q_ref, g_ref, kv0_ref, kv1_ref, att_ref, qg_ref, bg_ref):
    heads, near, pair = kv0_ref.shape[1:]
    width = pair // 2
    root = 1.0 / math.sqrt(width)
    lane = lax.broadcasted_iota(jnp.int32, (SPAN, pair), 1)
    left = lane < width
    zero = jnp.zeros((SPAN, pair), jnp.bfloat16)

    def dot(a, b, dims):
        return lax.dot_general(a, b, (dims, ((), ())), preferred_element_type=jnp.float32)

    def swap(a):
        return jnp.concatenate([a[:, width:], a[:, :width]], axis=1)

    def row(a, b):
        return jnp.concatenate([a, b], axis=1)

    for h in range(0, heads, 2):
        cols = slice(h * width, (h + 2) * width)
        q, g = q_ref[:, cols], g_ref[:, cols]
        kv = row(jnp.concatenate([kv0_ref[0, h], kv1_ref[0, h]], axis=0),
                 jnp.concatenate([kv0_ref[0, h + 1], kv1_ref[0, h + 1]], axis=0))
        both = jnp.concatenate([
            row(jnp.where(left, q, zero), zero),
            row(zero, jnp.where(left, swap(q), zero)),
            row(jnp.where(left, zero, swap(g)), zero),
            row(zero, jnp.where(left, zero, g)),
        ], axis=0)
        raw = dot(kv, both, ((1,), (1,)))
        score = raw[:, :pair] * root
        prob_grad = raw[:, pair:]
        weights = jnp.exp(score - jnp.max(score, axis=0, keepdims=True))
        probs = weights / jnp.sum(weights, axis=0, keepdims=True)
        low = probs.astype(jnp.bfloat16)
        term = jnp.sum(probs * prob_grad, axis=0, keepdims=True)
        sg = (probs * (prob_grad - term)).astype(jnp.bfloat16)
        applied = dot(row(low, sg), kv, ((0,), (0,)))
        at_a, at_b = applied[:SPAN, :pair], applied[SPAN:2 * SPAN, pair:]
        qg_a, qg_b = applied[2 * SPAN:3 * SPAN, :pair], applied[3 * SPAN:, pair:]
        att_ref[:, cols] = jnp.where(left, swap(at_a), at_b).astype(jnp.bfloat16)
        qg_ref[:, cols] = (jnp.where(left, qg_a, swap(qg_b)) * root).astype(jnp.bfloat16)
        back = dot(row(sg, low), both, ((1,), (0,)))
        scale = jnp.where(lax.broadcasted_iota(jnp.int32, back.shape, 1) % pair < width, root, 1.0)
        back = (back * scale).astype(jnp.bfloat16)
        for i in range(2):
            part = back[:, i * pair:(i + 1) * pair]
            bg_ref[0, h + i] = part[:near]
            bg_ref[1, h + i] = part[near:]


def attention(pos, queries, grads, blocks):
    rows, cols = queries.shape
    spans = rows // SPAN
    _, heads, near, pair = blocks.shape
    kv = lambda n: pl.BlockSpec((1, heads, near, pair), lambda i, pos: (pos[2 * i + n], 0, 0, 0))
    flat = pl.BlockSpec((SPAN, cols), lambda i, pos: (i, 0))
    return pl.pallas_call(
        attention_kernel,
        grid_spec=pltpu.PrefetchScalarGridSpec(
            num_scalar_prefetch=1,
            grid=(spans,),
            in_specs=[flat, flat, kv(0), kv(1)],
            out_specs=[flat, flat, pl.BlockSpec((2, heads, near, pair), lambda i, pos: (i, 0, 0, 0))],
        ),
        out_shape=[
            jax.ShapeDtypeStruct((rows, cols), jnp.bfloat16),
            jax.ShapeDtypeStruct((rows, cols), jnp.bfloat16),
            jax.ShapeDtypeStruct((2 * spans, heads, near, pair), jnp.bfloat16),
        ],
        compiler_params=pltpu.CompilerParams(vmem_limit_bytes=VMEM_LIMIT),
        name="attention",
    )(pos, queries, grads, blocks, blocks)


def gather_sum_kernel(code_ref, blk_ref, out_ref, acc):
    acc[...] = jnp.zeros_like(acc)

    def body(i, carry):
        code = code_ref[i]

        @pl.when(code >= 128)
        def _():
            e = code % 8
            for h in range(blk_ref.shape[1]):
                acc[e, h] += blk_ref[i, h].astype(jnp.float32)

        return carry

    lax.fori_loop(0, 64, body, 0)
    for e in range(8):
        out_ref[e] = jnp.swapaxes(acc[e], 0, 1)


def gather_sum(codes, blocks):
    _, heads, near, pair = blocks.shape
    return pl.pallas_call(
        gather_sum_kernel,
        in_specs=[pl.BlockSpec(memory_space=pltpu.SMEM), pl.BlockSpec(memory_space=pltpu.VMEM)],
        out_specs=pl.BlockSpec(memory_space=pltpu.VMEM),
        out_shape=jax.ShapeDtypeStruct((8, near, heads, pair), jnp.float32),
        scratch_shapes=[pltpu.VMEM((8, heads, near, pair), jnp.float32)],
        compiler_params=pltpu.CompilerParams(vmem_limit_bytes=VMEM_LIMIT),
        name="gather_sum",
    )(codes, blocks)


def slot_devices(me):
    y, z, c = me // (2 * NZ), (me // 2) % NZ, me % 2
    ys = jnp.array([j[0] for j in J_OFF], jnp.int32)[:, None]
    cs = jnp.array([j[1] for j in J_OFF], jnp.int32)[:, None]
    zs = jnp.array(Z_OFF, jnp.int32)[None, :]
    return dp_of((y + ys + NY) % NY, (z + zs + NZ) % NZ, (c + cs) % 2).reshape(-1)


def on_device(tokens, query_weight, neighbour_store, neighbours, attended_grad):
    entries_here, near, heads, pair = neighbour_store.shape
    me = lax.axis_index("dp")
    refs = neighbours.reshape(64, -1)
    order = jnp.arange(refs.shape[1], dtype=jnp.int32)[None, :]
    word = 128 + 8 * order + refs % entries_here
    shard = jnp.arange(64, dtype=jnp.int32)
    table = jnp.max(
        jnp.where((refs // entries_here)[:, :, None] == shard, word[:, :, None], 0), axis=1)
    code = table.reshape(-1)

    slots = slot_devices(me)
    mine = lax.dynamic_index_in_dim(refs, me, 0, keepdims=False) // entries_here
    pos = jnp.sum(
        jnp.where(mine[:, None] == slots[None, :], jnp.arange(64, dtype=jnp.int32)[None, :], 0), axis=1)

    store = neighbour_store.transpose(0, 2, 1, 3).reshape(entries_here, 2, heads * near // 2, pair)
    got, queries = exchange_out(code, store, tokens, query_weight)
    got = got.reshape(64, heads, near, pair)
    attended, query_grad, block_grad = attention(pos, queries, attended_grad, got)
    halves = block_grad.reshape(-1, 2, heads * near // 2, pair)
    back, token_grad, weight_share = exchange_back(code, halves, query_grad, tokens, query_weight)
    weight_grad = weight_share.T
    column = jnp.take(table, slots, axis=0)
    column = lax.dynamic_index_in_dim(column, me, 1, keepdims=False)
    store_grad = gather_sum(column, back.reshape(64, heads, near, pair))
    return (attended, token_grad, weight_grad, store_grad)


def solution(mesh):
    return jax.shard_map(
        on_device,
        mesh=mesh,
        in_specs=(
            P("dp", "fsdp"),
            P("fsdp", None),
            P("dp", None, "fsdp", None),
            P(),
            P("dp", "fsdp"),
        ),
        out_specs=(P("dp", "fsdp"), P("dp", "fsdp"), P("fsdp", "dp"), P("dp", None, "fsdp", None)),
        check_vma=False,
    )
```

```python
import functools
import math

import jax
import jax.numpy as jnp
from jax import lax
from jax.experimental import pallas as pl
from jax.experimental.pallas import tpu as pltpu
from jax.sharding import PartitionSpec as P

SPAN = 64
NY, NZ = 4, 8
MESH = pl.DeviceIdType.MESH
Z_OFF = (0, -1, 1, -2, 2, -3, 3, 4)
J_OFF = ((0, 0), (0, 1), (-1, 0), (-1, 1), (1, 0), (1, 1), (2, 0), (2, 1))
VMEM_LIMIT = 60 * 1024 * 1024


def dp_of(y, z, c):
    return (y * NZ + z) * 2 + c


class Place:
    def __init__(self):
        me = lax.axis_index("dp")
        self.x = lax.axis_index("fsdp")
        self.y, self.z, self.c = me // (2 * NZ), (me // 2) % NZ, me % 2

    def dp(self, dy, dz, dc):
        return dp_of((self.y + dy + NY) % NY, (self.z + dz + NZ) % NZ, (self.c + dc) % 2)

    def dev(self, dy=0, dz=0, dc=0, dx=0):
        return (self.dp(dy, dz, dc), (self.x + dx + 4) % 4)


def greet(devices):
    barrier = pltpu.get_barrier_semaphore()
    for d in devices:
        pl.semaphore_signal(barrier, inc=1, device_id=d, device_id_type=MESH)
    pl.semaphore_wait(barrier, len(devices))


def remote(src, dst, ssem, rsem, d):
    return pltpu.make_async_remote_copy(
        src_ref=src, dst_ref=dst, send_sem=ssem, recv_sem=rsem, device_id=d, device_id_type=MESH)


def plane_partners(p):
    return [p.dev(dy, 0, dc) for dy, dc in J_OFF[1:]]


SLOTS = ((1, 1), (6, 6), (7, 7), (4, 2), (5, 3), (2, 4), (3, 5))


def plane_send(p, out, k, hh, blocks, ysend, yrecv, ls):
    local = pltpu.make_async_copy(blocks(0), out.at[k, hh], ls.at[k, hh])
    local.start()
    sends = []
    for i, j in SLOTS:
        dy, dc = J_OFF[i]
        cp = remote(blocks(i), out.at[j * 8 + k, hh], ysend.at[k, hh, i], yrecv.at[j * 8 + k, hh],
                    p.dev(dy, 0, dc))
        cp.start()
        sends.append(cp)
    return local, sends


def attend(q, g, kv, root):
    pair = q.shape[1]
    width = pair // 2
    left = lax.broadcasted_iota(jnp.int32, q.shape, 1) < width
    zero = jnp.zeros(q.shape, q.dtype)

    def dot(a, b, dims):
        return lax.dot_general(a, b, (dims, ((), ())), preferred_element_type=jnp.float32)

    def swap(a):
        return jnp.concatenate([a[:, width:], a[:, :width]], axis=1)

    def row(a, b):
        return jnp.concatenate([a, b], axis=1)

    both = jnp.concatenate([
        row(jnp.where(left, q, zero), zero),
        row(zero, jnp.where(left, swap(q), zero)),
        row(jnp.where(left, zero, swap(g)), zero),
        row(zero, jnp.where(left, zero, g)),
    ], axis=0)
    raw = dot(kv, both, ((1,), (1,)))
    score = raw[:, :pair] * root
    prob_grad = raw[:, pair:]
    weights = jnp.exp(score - jnp.max(score, axis=0, keepdims=True))
    probs = weights / jnp.sum(weights, axis=0, keepdims=True)
    low = probs.astype(jnp.bfloat16)
    term = jnp.sum(probs * prob_grad, axis=0, keepdims=True)
    sg = (probs * (prob_grad - term)).astype(jnp.bfloat16)
    applied = dot(row(low, sg), kv, ((0,), (0,)))
    at_a, at_b = applied[:SPAN, :pair], applied[SPAN:2 * SPAN, pair:]
    qg_a, qg_b = applied[2 * SPAN:3 * SPAN, :pair], applied[3 * SPAN:, pair:]
    attended = jnp.where(left, swap(at_a), at_b).astype(jnp.bfloat16)
    query_grad = (jnp.where(left, qg_a, swap(qg_b)) * root).astype(jnp.bfloat16)
    back = dot(row(sg, low), both, ((1,), (0,)))
    scale = jnp.where(lax.broadcasted_iota(jnp.int32, back.shape, 1) % pair < width, root, 1.0)
    return attended, query_grad, (back * scale).astype(jnp.bfloat16)


def whole_kernel(near, code_ref, pos_ref, own, tokens_far, weight_far, grads_far,
                 out, attended, token_grad, wout,
                 fp0, fp1, fp2, fm0, fm1, fm2, f4, sbuf, brought, tokens, weight, grads,
                 q_a, q_b, q_up, q_dn, queries, bg,
                 zp0, zp1, zm0, zm1, zp2, zm2, z4, gathered, share, crecv, s_own,
                 y_a, y_b, y_up, y_dn, w_up1, w_up, w_dn1, w_dn,
                 fetch, fs, fr, fysend, fyrecv, qs, qr,
                 zs, zr, zs4, zr4, ysend, yrecv, ls, xs, xr, cs, cr, ws, wr, us, ur):
    p = Place()
    fetches = [pltpu.make_async_copy(tokens_far, tokens, fetch.at[0]),
               pltpu.make_async_copy(weight_far, weight, fetch.at[1]),
               pltpu.make_async_copy(grads_far, grads, fetch.at[2])]
    for cp in fetches:
        cp.start()
    up, down = p.dev(0, 1), p.dev(0, -1)
    yup, ydn = p.dev(1), p.dev(-1)
    xup, xdn, xfar = p.dev(dx=1), p.dev(dx=-1), p.dev(dx=2)
    greet([up, down, xup, xdn, xfar] + plane_partners(p))

    entries = own.shape[0]
    lo, hi = pl.ds(0, entries // 2), pl.ds(entries // 2, entries // 2)
    fups, fdowns = [], []
    for hh in range(2):
        fups.append([remote(own.at[:, hh], fp0[hh], fs.at[0, hh], fr.at[0, hh], up),
                     remote(fp0[hh], fp1[hh], fs.at[1, hh], fr.at[1, hh], up),
                     remote(fp1[hh], fp2[hh], fs.at[2, hh], fr.at[2, hh], up),
                     remote(fp2[hh].at[lo], f4[hh].at[lo], fs.at[3, hh], fr.at[3, hh], up)])
        fdowns.append([remote(own.at[:, hh], fm0[hh], fs.at[4, hh], fr.at[4, hh], down),
                       remote(fm0[hh], fm1[hh], fs.at[5, hh], fr.at[5, hh], down),
                       remote(fm1[hh], fm2[hh], fs.at[6, hh], fr.at[6, hh], down),
                       remote(fm2[hh].at[hi], f4[hh].at[hi], fs.at[7, hh], fr.at[7, hh], down)])
    fsets = [None, fp0, fm0, fp1, fm1, fp2, fm2, f4]
    fsent = [[], []]

    def bring(k, hh):
        origin = p.dp(0, Z_OFF[k], 0)

        def block(i):
            dy, dc = J_OFF[i]
            e = code_ref[p.dp(dy, 0, dc) * 64 + origin] % 8
            return own[e, hh] if k == 0 else fsets[k][hh][e]

        brought[hh][k] = block(0)
        for i, j in SLOTS:
            dy, dc = J_OFF[i]
            sbuf[k, hh, i] = block(i)
            cp = remote(sbuf.at[k, hh, i], brought[hh].at[j * 8 + k], fysend.at[k, hh, i],
                        fyrecv.at[j * 8 + k, hh], p.dev(dy, 0, dc))
            cp.start()
            fsent[hh].append(cp)

    for hh in range(2):
        fups[hh][0].start()
        fdowns[hh][0].start()
    for hh in range(2):
        bring(0, hh)

    for cp in fetches:
        cp.wait()
    rows, width = queries.shape
    half = rows // 2
    parts = [share.at[n, :, pl.ds(0, width)] for n in range(4)]
    for n, dx in enumerate((2, 1, -1, 0)):
        cols = pl.ds(pl.multiple_of((p.x + dx + 4) % 4 * width, width), width)

        @pl.loop(0, 4)
        def _(r, n=n, cols=cols):
            some = pl.ds(pl.multiple_of(r * (rows // 4), rows // 4), rows // 4)
            share[n, some, :width] = jnp.dot(
                tokens[some, :], weight[:, cols], preferred_element_type=jnp.float32)

        if n == 0:
            qfar_up = remote(share.at[0, pl.ds(0, half), pl.ds(0, width)], q_a, qs.at[0], qr.at[0], xup)
            qfar_dn = remote(share.at[0, pl.ds(half, half), pl.ds(0, width)], q_b, qs.at[1], qr.at[1], xdn)
            qfar_up.start()
            qfar_dn.start()

    qnear_up = remote(parts[1], q_up, qs.at[2], qr.at[2], xup)
    qnear_dn = remote(parts[2], q_dn, qs.at[3], qr.at[3], xdn)
    for s in range(3):
        for hh in range(2):
            fups[hh][s].wait_recv()
            fups[hh][s + 1].start()
            fdowns[hh][s].wait_recv()
            fdowns[hh][s + 1].start()
            bring(1 + 2 * s, hh)
            bring(2 + 2 * s, hh)
        if s == 0:
            qfar_up.wait_recv()
            share[1, :half, :width] += q_a[...]
            qnear_up.start()
            qfar_dn.wait_recv()
            share[2, half:, :width] += q_b[...]
            qnear_dn.start()
    for hh in range(2):
        fups[hh][3].wait_recv()
        fdowns[hh][3].wait_recv()
        bring(7, hh)
    qnear_up.wait_recv()
    qnear_dn.wait_recv()
    queries[...] = (share[3, :, :width] + q_up[...] + q_dn[...]).astype(queries.dtype)
    for cp in (qfar_up, qfar_dn, qnear_up, qnear_dn):
        cp.wait_send()

    pair = own.shape[-1]
    root = 1.0 / math.sqrt(pair // 2)
    heads = own.shape[2] // near
    ups, downs = [], []
    for hh in range(2):
        ups.append([remote(bg[hh], zp0[hh], zs.at[0, hh], zr.at[0, hh], up),
                    remote(zp0[hh], zp1[hh], zs.at[1, hh], zr.at[1, hh], up),
                    remote(sbuf.at[5, hh], zp2.at[hh, pl.ds(0, 8)], zs.at[2, hh], zr.at[2, hh], up),
                    remote(zp2.at[hh, pl.ds(8, 4)], z4.at[hh, pl.ds(0, 4)], zs.at[3, hh], zr.at[3, hh], up),
                    remote(sbuf.at[7, hh, pl.ds(0, 4)], zp2.at[hh, pl.ds(8, 4)], zs4.at[0, hh], zr4.at[0, hh], up)])
        downs.append([remote(bg[hh], zm0[hh], zs.at[4, hh], zr.at[4, hh], down),
                      remote(zm0[hh], zm1[hh], zs.at[5, hh], zr.at[5, hh], down),
                      remote(sbuf.at[6, hh], zm2.at[hh, pl.ds(0, 8)], zs.at[6, hh], zr.at[6, hh], down),
                      remote(zm2.at[hh, pl.ds(8, 4)], z4.at[hh, pl.ds(4, 4)], zs.at[7, hh], zr.at[7, hh], down),
                      remote(sbuf.at[7, hh, pl.ds(4, 4)], zm2.at[hh, pl.ds(8, 4)], zs4.at[1, hh], zr4.at[1, hh], down)])
    sets = [None, zp0, zm0, zp1, zm1]
    started, gathers = [], []

    def pick(origin, target):
        return (code_ref[origin * 64 + target] // 8) % 16

    def process(k, hh):
        origin = p.dp(0, Z_OFF[k], 0)
        for i, (dy, dc) in enumerate(J_OFF):
            r = pick(origin, p.dp(dy, 0, dc))
            sbuf[k, hh, i] = bg[hh][r] if k == 0 else sets[k][hh][r]
        started.append(plane_send(p, out, k, hh, lambda i: sbuf.at[k, hh, i], ysend, yrecv, ls))

    def forward(k, hh, buf):
        started.append(plane_send(p, out, k, hh, lambda i: buf.at[hh, i], ysend, yrecv, ls))

    def stage(hh, held, place, way, part):
        origin = p.dp(0, -2 * way, 0)
        for i, (dy, dc) in enumerate(J_OFF):
            sbuf[place, hh, i] = held[hh][pick(origin, p.dp(dy, way, dc))]
        for i in range(4):
            dy, dc = J_OFF[part + i]
            sbuf[7, hh, part + i] = held[hh][pick(origin, p.dp(dy, 2 * way, dc))]

    for hh in range(2):
        for cp in fsent[hh]:
            cp.wait()

        @pl.loop(0, rows // SPAN // 2)
        def _(step, hh=hh):
            for sub in range(2):
                span = step * 2 + sub
                some = pl.ds(pl.multiple_of(span * SPAN, SPAN), SPAN)
                kv0, kv1 = brought[hh][pos_ref[2 * span]], brought[hh][pos_ref[2 * span + 1]]
                for i in range(0, heads, 2):
                    first = (hh * heads + i) * (pair // 2)
                    cols = slice(first, first + pair)
                    kv = jnp.concatenate([
                        jnp.concatenate([kv0[h * near:(h + 1) * near], kv1[h * near:(h + 1) * near]], axis=0)
                        for h in (i, i + 1)], axis=1)
                    at, qg, back = attend(queries[some, cols], grads[some, cols], kv, root)
                    attended[some, cols] = at
                    gathered[p.x, some, cols] = qg
                    for h in range(2):
                        lanes = slice(h * pair, (h + 1) * pair)
                        place = slice((i + h) * near, (i + h + 1) * near)
                        bg[hh][2 * span, place, :] = back[:near, lanes]
                        bg[hh][2 * span + 1, place, :] = back[near:, lanes]

        ups[hh][0].start()
        downs[hh][0].start()
        mine = gathered.at[p.x, :, pl.ds(hh * half, half)]
        for i, d in enumerate((xup, xdn, xfar)):
            cp = remote(mine, mine, xs.at[i, hh], xr.at[i, hh], d)
            cp.start()
            gathers.append(cp)
        process(0, hh)

    def hop1(hh):
        ups[hh][0].wait_recv()
        ups[hh][1].start()
        downs[hh][0].wait_recv()
        downs[hh][1].start()
        process(1, hh)
        process(2, hh)

    hop1(0)
    for cp in gathers:
        cp.wait_recv()

    tn = (((0,), (0,)), ((), ()))
    nt = (((1,), (1,)), ((), ()))
    chunk = 32 * NZ
    kept = p.c * chunk
    pairs = []
    for n, dy in enumerate((2, 1, -1, 0)):
        yy = (p.y + dy + NY) % NY

        @pl.loop(0, 2)
        def _(r, yy=yy, n=n):
            cols = pl.ds(pl.multiple_of(r * chunk, chunk), chunk)
            part = lax.dot_general(gathered[yy, :, cols], tokens[...], tn, preferred_element_type=jnp.float32)
            part = part.reshape(NZ // 2, 2, 32, part.shape[1])
            for core in range(2):
                share[n, pl.ds(pl.multiple_of(core * chunk + r * (chunk // 2), chunk // 2), chunk // 2)] = (
                    part[:, core].reshape(chunk // 2, part.shape[3]))

        cp = remote(share.at[n, pl.ds(pl.multiple_of(chunk - kept, chunk), chunk)], crecv.at[n],
                    cs.at[n], cr.at[n], p.dev(0, 0, 1))
        cp.start()
        pairs.append(cp)

    hop1(1)

    def held(i, count=32):
        return pl.ds(pl.multiple_of(kept + i * 32, 32), count)

    def lump(i):
        return pl.ds(pl.multiple_of(i * 32, 32), 32)

    for n in range(4):
        pairs[n].wait_recv()

        @pl.loop(0, NZ)
        def _(i, n=n):
            share[n, held(i)] += crecv[n, lump(i)]

        if n == 0:
            far_up = remote(share.at[0, held(0, chunk // 2)], y_a, ws.at[0], wr.at[0], yup)
            far_dn = remote(share.at[0, held(4, chunk // 2)], y_b, ws.at[1], wr.at[1], ydn)
            far_up.start()
            far_dn.start()

    @pl.loop(0, 4)
    def _(i):
        some = pl.ds(pl.multiple_of(i * 128, 128), 128)
        total = jnp.zeros((128, weight.shape[0]), jnp.float32)
        for a in range(4):
            total += lax.dot_general(gathered[a, some, :], weight[:, a * 512:(a + 1) * 512], nt,
                                     preferred_element_type=jnp.float32)
        token_grad[some, :] = total.astype(token_grad.dtype)

    far_up.wait_recv()

    @pl.loop(0, 4)
    def _(i):
        share[1, held(i)] += y_a[lump(i)]

    near_up = remote(share.at[1, held(0, chunk)], y_up, ws.at[2], wr.at[2], yup)
    near_up.start()
    far_dn.wait_recv()

    @pl.loop(0, 4)
    def _(i):
        share[2, held(i + 4)] += y_b[lump(i)]

    near_dn = remote(share.at[2, held(0, chunk)], y_dn, ws.at[3], wr.at[3], ydn)
    near_dn.start()

    def hop2(hh):
        ups[hh][1].wait_recv()
        stage(hh, zp1, 5, 1, 0)
        ups[hh][2].start()
        ups[hh][4].start()
        downs[hh][1].wait_recv()
        stage(hh, zm1, 6, -1, 4)
        downs[hh][2].start()
        downs[hh][4].start()
        process(3, hh)
        process(4, hh)

    def hop3(hh):
        ups[hh][4].wait_recv()
        ups[hh][3].start()
        downs[hh][4].wait_recv()
        downs[hh][3].start()
        ups[hh][2].wait_recv()
        forward(5, hh, zp2)
        downs[hh][2].wait_recv()
        forward(6, hh, zm2)

    def hop4(hh):
        ups[hh][3].wait_recv()
        downs[hh][3].wait_recv()
        forward(7, hh, z4)

    hop2(0)
    hop2(1)
    near_up.wait_recv()
    near_dn.wait_recv()

    @pl.loop(0, NZ)
    def _(i):
        s_own[i] = share[3, held(i)] + y_up[lump(i)] + y_dn[lump(i)]

    def at(dz):
        return (p.z + dz + NZ) % NZ

    chain_up = [remote(s_own.at[at(4), pl.ds(0, 16)], w_up1, us.at[0], ur.at[0], up)]
    chain_dn = [remote(s_own.at[at(4), pl.ds(16, 16)], w_dn1, us.at[4], ur.at[4], down)]
    for i, dz in enumerate((3, 2, 1)):
        chain_up.append(remote(s_own.at[at(dz)], w_up.at[i], us.at[1 + i], ur.at[1 + i], up))
        chain_dn.append(remote(s_own.at[at(-dz)], w_dn.at[i], us.at[5 + i], ur.at[5 + i], down))

    def ring(step):
        if step == 1:
            chain_up[0].wait_recv()
            s_own[at(3), pl.ds(0, 16)] += w_up1[...]
            chain_dn[0].wait_recv()
            s_own[at(-3), pl.ds(16, 16)] += w_dn1[...]
        elif step > 1:
            chain_up[step - 1].wait_recv()
            s_own[at(4 - step)] += w_up[step - 2]
            chain_dn[step - 1].wait_recv()
            s_own[at(step - 4)] += w_dn[step - 2]
        if step < 4:
            chain_up[step].start()
            chain_dn[step].start()

    ring(0)
    hop3(0)
    ring(1)
    hop3(1)
    ring(2)
    hop4(0)
    ring(3)
    hop4(1)
    chain_up[3].wait_recv()
    chain_dn[3].wait_recv()
    wout[...] = s_own[p.z] + w_up[2] + w_dn[2]

    for local, sends in started:
        local.wait()
        for cp in sends:
            cp.wait()
    for hh in range(2):
        for cp in fups[hh] + fdowns[hh] + ups[hh] + downs[hh]:
            cp.wait_send()
    for cp in gathers + pairs + [far_up, far_dn, near_up, near_dn] + chain_up + chain_dn:
        cp.wait_send()


def whole(near, code, pos, own, tokens, weight, grads):
    n, _, rows, cols = own.shape
    toks, feats = tokens.shape
    width = weight.shape[1] // 4
    low, full = jnp.bfloat16, jnp.float32
    refs = 16
    chunk = 32 * NZ
    blocks = lambda count: [pltpu.VMEM((count, rows, cols), low)] * 2
    halves = lambda count: pltpu.VMEM((2, count, rows, cols), low)
    wide = lambda *lead: pltpu.VMEM(lead + (feats,), full)
    flat = lambda count: pltpu.VMEM((count, width), full)
    dma = pltpu.SemaphoreType.DMA
    vmem = pl.BlockSpec(memory_space=pltpu.VMEM)
    smem = pl.BlockSpec(memory_space=pltpu.SMEM)
    hbm = pl.BlockSpec(memory_space=pl.ANY)
    return pl.pallas_call(
        functools.partial(whole_kernel, near),
        out_shape=[
            jax.ShapeDtypeStruct((64, 2, rows, cols), low),
            jax.ShapeDtypeStruct((toks, width), low),
            jax.ShapeDtypeStruct((toks, feats), low),
            jax.ShapeDtypeStruct((32, feats), full),
        ],
        in_specs=[smem, smem, vmem, hbm, hbm, hbm],
        out_specs=[hbm, vmem, vmem, vmem],
        scratch_shapes=[blocks(n)] * 7 + [
            pltpu.VMEM((8, 2, 8, rows, cols), low),
            blocks(64),
            pltpu.VMEM(tokens.shape, low), pltpu.VMEM(weight.shape, low), pltpu.VMEM(grads.shape, low),
            flat(toks // 2), flat(toks // 2), flat(toks), flat(toks),
            pltpu.VMEM((toks, width), low),
            blocks(refs), blocks(refs), blocks(refs), blocks(refs), blocks(refs),
            halves(12), halves(12), halves(8),
            pltpu.VMEM((4, toks, width), low),
            wide(4, 2 * chunk), wide(4, chunk), wide(NZ, 32),
            wide(chunk // 2), wide(chunk // 2), wide(chunk), wide(chunk),
            wide(16), wide(3, 32), wide(16), wide(3, 32),
            dma((3,)), dma((8, 2)), dma((8, 2)), dma((8, 2, 8)), dma((64, 2)), dma((4,)), dma((4,)),
            dma((8, 2)), dma((8, 2)), dma((2, 2)), dma((2, 2)), dma((8, 2, 8)), dma((64, 2)), dma((8, 2)),
            dma((3, 2)), dma((3, 2)), dma((4,)), dma((4,)), dma((4,)), dma((4,)), dma((8,)), dma((8,)),
        ],
        compiler_params=pltpu.CompilerParams(
            collective_id=0, has_side_effects=True, vmem_limit_bytes=VMEM_LIMIT),
        cost_estimate=pl.CostEstimate(flops=0, bytes_accessed=500_000_000, transcendentals=0),
        name="whole",
    )(code, pos, own, tokens, weight, grads)


def gather_sum_kernel(code_ref, blk_ref, out_ref, acc):
    acc[...] = jnp.zeros_like(acc)

    def body(i, carry):
        code = code_ref[i]

        @pl.when(code >= 128)
        def _():
            e = code % 8
            for h in range(blk_ref.shape[1]):
                acc[e, h] += blk_ref[i, h].astype(jnp.float32)

        return carry

    lax.fori_loop(0, 64, body, 0)
    for e in range(8):
        out_ref[e] = jnp.swapaxes(acc[e], 0, 1)


def gather_sum(codes, blocks):
    _, heads, near, pair = blocks.shape
    return pl.pallas_call(
        gather_sum_kernel,
        in_specs=[pl.BlockSpec(memory_space=pltpu.SMEM), pl.BlockSpec(memory_space=pltpu.VMEM)],
        out_specs=pl.BlockSpec(memory_space=pltpu.VMEM),
        out_shape=jax.ShapeDtypeStruct((8, near, heads, pair), jnp.float32),
        scratch_shapes=[pltpu.VMEM((8, heads, near, pair), jnp.float32)],
        compiler_params=pltpu.CompilerParams(vmem_limit_bytes=VMEM_LIMIT),
        name="gather_sum",
    )(codes, blocks)


def slot_devices(me):
    y, z, c = me // (2 * NZ), (me // 2) % NZ, me % 2
    ys = jnp.array([j[0] for j in J_OFF], jnp.int32)[:, None]
    cs = jnp.array([j[1] for j in J_OFF], jnp.int32)[:, None]
    zs = jnp.array(Z_OFF, jnp.int32)[None, :]
    return dp_of((y + ys + NY) % NY, (z + zs + NZ) % NZ, (c + cs) % 2).reshape(-1)


def on_device(tokens, query_weight, neighbour_store, neighbours, attended_grad):
    entries_here, near, heads, pair = neighbour_store.shape
    me = lax.axis_index("dp")
    refs = neighbours.reshape(64, -1)
    order = jnp.arange(refs.shape[1], dtype=jnp.int32)[None, :]
    word = 128 + 8 * order + refs % entries_here
    shard = jnp.arange(64, dtype=jnp.int32)
    table = jnp.max(
        jnp.where((refs // entries_here)[:, :, None] == shard, word[:, :, None], 0), axis=1)
    code = table.reshape(-1)

    slots = slot_devices(me)
    mine = lax.dynamic_index_in_dim(refs, me, 0, keepdims=False) // entries_here
    pos = jnp.sum(
        jnp.where(mine[:, None] == slots[None, :], jnp.arange(64, dtype=jnp.int32)[None, :], 0), axis=1)

    store = neighbour_store.transpose(0, 2, 1, 3).reshape(entries_here, 2, heads * near // 2, pair)
    back, attended, token_grad, weight_share = whole(
        near, code, pos, store, tokens, query_weight, attended_grad)
    weight_grad = weight_share.T
    column = jnp.take(table, slots, axis=0)
    column = lax.dynamic_index_in_dim(column, me, 1, keepdims=False)
    store_grad = gather_sum(column, back.reshape(64, heads, near, pair))
    return (attended, token_grad, weight_grad, store_grad)


def solution(mesh):
    return jax.shard_map(
        on_device,
        mesh=mesh,
        in_specs=(
            P("dp", "fsdp"),
            P("fsdp", None),
            P("dp", None, "fsdp", None),
            P(),
            P("dp", "fsdp"),
        ),
        out_specs=(P("dp", "fsdp"), P("dp", "fsdp"), P("fsdp", "dp"), P("dp", None, "fsdp", None)),
        check_vma=False,
    )
```

```python
import functools
import math

import jax
import jax.numpy as jnp
from jax import lax
from jax.experimental import pallas as pl
from jax.experimental.pallas import tpu as pltpu
from jax.sharding import PartitionSpec as P

SPAN = 64
PARTS = 4
NY, NZ = 4, 8
MESH = pl.DeviceIdType.MESH
Z_OFF = (0, -1, 1, -2, 2, -3, 3, 4)
J_OFF = ((0, 0), (0, 1), (-1, 0), (-1, 1), (1, 0), (1, 1), (2, 0), (2, 1))
VMEM_LIMIT = 60 * 1024 * 1024


def dp_of(y, z, c):
    return (y * NZ + z) * 2 + c


class Place:
    def __init__(self):
        me = lax.axis_index("dp")
        self.x = lax.axis_index("fsdp")
        self.y, self.z, self.c = me // (2 * NZ), (me // 2) % NZ, me % 2

    def dp(self, dy, dz, dc):
        return dp_of((self.y + dy + NY) % NY, (self.z + dz + NZ) % NZ, (self.c + dc) % 2)

    def dev(self, dy=0, dz=0, dc=0, dx=0):
        return (self.dp(dy, dz, dc), (self.x + dx + 4) % 4)


def greet(devices):
    barrier = pltpu.get_barrier_semaphore()
    for d in devices:
        pl.semaphore_signal(barrier, inc=1, device_id=d, device_id_type=MESH)
    pl.semaphore_wait(barrier, len(devices))


def remote(src, dst, ssem, rsem, d):
    return pltpu.make_async_remote_copy(
        src_ref=src, dst_ref=dst, send_sem=ssem, recv_sem=rsem, device_id=d, device_id_type=MESH)


def plane_partners(p):
    return [p.dev(dy, 0, dc) for dy, dc in J_OFF[1:]]


SLOTS = ((1, 1), (6, 6), (7, 7), (4, 2), (5, 3), (2, 4), (3, 5))


def plane_send(p, out, k, hh, blocks, ysend, yrecv, ls):
    local = pltpu.make_async_copy(blocks(0), out.at[k, hh], ls.at[k, hh])
    local.start()
    sends = []
    for i, j in SLOTS:
        dy, dc = J_OFF[i]
        cp = remote(blocks(i), out.at[j * 8 + k, hh], ysend.at[k, hh, i], yrecv.at[j * 8 + k, hh],
                    p.dev(dy, 0, dc))
        cp.start()
        sends.append(cp)
    return local, sends


def attend(q, g, kv, root):
    pair = q.shape[1]
    width = pair // 2
    left = lax.broadcasted_iota(jnp.int32, q.shape, 1) < width
    zero = jnp.zeros(q.shape, q.dtype)

    def dot(a, b, dims):
        return lax.dot_general(a, b, (dims, ((), ())), preferred_element_type=jnp.float32)

    def swap(a):
        return jnp.concatenate([a[:, width:], a[:, :width]], axis=1)

    def row(a, b):
        return jnp.concatenate([a, b], axis=1)

    both = jnp.concatenate([
        row(jnp.where(left, q, zero), zero),
        row(zero, jnp.where(left, swap(q), zero)),
        row(jnp.where(left, zero, swap(g)), zero),
        row(zero, jnp.where(left, zero, g)),
    ], axis=0)
    raw = dot(kv, both, ((1,), (1,)))
    score = raw[:, :pair] * root
    prob_grad = raw[:, pair:]
    weights = jnp.exp(score - jnp.max(score, axis=0, keepdims=True))
    probs = weights / jnp.sum(weights, axis=0, keepdims=True)
    low = probs.astype(jnp.bfloat16)
    term = jnp.sum(probs * prob_grad, axis=0, keepdims=True)
    sg = (probs * (prob_grad - term)).astype(jnp.bfloat16)
    applied = dot(row(low, sg), kv, ((0,), (0,)))
    at_a, at_b = applied[:SPAN, :pair], applied[SPAN:2 * SPAN, pair:]
    qg_a, qg_b = applied[2 * SPAN:3 * SPAN, :pair], applied[3 * SPAN:, pair:]
    attended = jnp.where(left, swap(at_a), at_b).astype(jnp.bfloat16)
    query_grad = (jnp.where(left, qg_a, swap(qg_b)) * root).astype(jnp.bfloat16)
    back = dot(row(sg, low), both, ((1,), (0,)))
    scale = jnp.where(lax.broadcasted_iota(jnp.int32, back.shape, 1) % pair < width, root, 1.0)
    return attended, query_grad, (back * scale).astype(jnp.bfloat16)


def whole_kernel(near, code_ref, refs_ref, own, tokens_far, weight_far, grads_far,
                 out, attended, token_grad, wout,
                 fp0, fp1, fp2, fm0, fm1, fm2, f4, sbuf, brought, tokens, weight, grads,
                 q_a, q_b, q_up, q_dn, queries, bg,
                 zp0, zp1, zm0, zm1, zp2, zm2, z4, gathered, share, crecv, s_own,
                 y_a, y_b, y_up, y_dn, w_up1, w_up, w_dn1, w_dn,
                 fetch, fs, fr, fysend, fyrecv, qs, qr,
                 zs, zr, zs4, zr4, ysend, yrecv, ls, xs, xr, cs, cr, ws, wr, us, ur):
    p = Place()
    fetches = [pltpu.make_async_copy(tokens_far, tokens, fetch.at[0]),
               pltpu.make_async_copy(weight_far, weight, fetch.at[1]),
               pltpu.make_async_copy(grads_far, grads, fetch.at[2])]
    for cp in fetches:
        cp.start()
    up, down = p.dev(0, 1), p.dev(0, -1)
    yup, ydn = p.dev(1), p.dev(-1)
    xup, xdn, xfar = p.dev(dx=1), p.dev(dx=-1), p.dev(dx=2)
    greet([up, down, xup, xdn, xfar] + plane_partners(p))

    entries = own.shape[0]
    lo, hi = pl.ds(0, entries // 2), pl.ds(entries // 2, entries // 2)
    fups, fdowns = [], []
    for hh in range(PARTS):
        fups.append([remote(own.at[:, hh], fp0[hh], fs.at[0, hh], fr.at[0, hh], up),
                     remote(fp0[hh], fp1[hh], fs.at[1, hh], fr.at[1, hh], up),
                     remote(fp1[hh], fp2[hh], fs.at[2, hh], fr.at[2, hh], up),
                     remote(fp2[hh].at[lo], f4[hh].at[lo], fs.at[3, hh], fr.at[3, hh], up)])
        fdowns.append([remote(own.at[:, hh], fm0[hh], fs.at[4, hh], fr.at[4, hh], down),
                       remote(fm0[hh], fm1[hh], fs.at[5, hh], fr.at[5, hh], down),
                       remote(fm1[hh], fm2[hh], fs.at[6, hh], fr.at[6, hh], down),
                       remote(fm2[hh].at[hi], f4[hh].at[hi], fs.at[7, hh], fr.at[7, hh], down)])
    fsets = [None, fp0, fm0, fp1, fm1, fp2, fm2, f4]
    fsent = [[] for _ in range(PARTS)]

    def bring(k, hh):
        origin = p.dp(0, Z_OFF[k], 0)

        def block(i):
            dy, dc = J_OFF[i]
            e = code_ref[p.dp(dy, 0, dc) * 64 + origin] % 8
            return own[e, hh] if k == 0 else fsets[k][hh][e]

        brought[hh][k] = block(0)
        for i, j in SLOTS:
            dy, dc = J_OFF[i]
            sbuf[k, hh, i] = block(i)
            cp = remote(sbuf.at[k, hh, i], brought[hh].at[j * 8 + k], fysend.at[k, hh, i],
                        fyrecv.at[j * 8 + k, hh], p.dev(dy, 0, dc))
            cp.start()
            fsent[hh].append(cp)

    for hh in range(PARTS):
        fups[hh][0].start()
        fdowns[hh][0].start()
    for hh in range(PARTS):
        bring(0, hh)

    for cp in fetches:
        cp.wait()
    rows, width = queries.shape
    half = rows // 2
    parts = [share.at[n, :, pl.ds(0, width)] for n in range(4)]
    for n, dx in enumerate((2, 1, -1, 0)):
        cols = pl.ds(pl.multiple_of((p.x + dx + 4) % 4 * width, width), width)

        @pl.loop(0, 4)
        def _(r, n=n, cols=cols):
            some = pl.ds(pl.multiple_of(r * (rows // 4), rows // 4), rows // 4)
            share[n, some, :width] = jnp.dot(
                tokens[some, :], weight[:, cols], preferred_element_type=jnp.float32)

        if n == 0:
            qfar_up = remote(share.at[0, pl.ds(0, half), pl.ds(0, width)], q_a, qs.at[0], qr.at[0], xup)
            qfar_dn = remote(share.at[0, pl.ds(half, half), pl.ds(0, width)], q_b, qs.at[1], qr.at[1], xdn)
            qfar_up.start()
            qfar_dn.start()

    qnear_up = remote(parts[1], q_up, qs.at[2], qr.at[2], xup)
    qnear_dn = remote(parts[2], q_dn, qs.at[3], qr.at[3], xdn)
    for s in range(3):
        for hh in range(PARTS):
            fups[hh][s].wait_recv()
            fups[hh][s + 1].start()
            fdowns[hh][s].wait_recv()
            fdowns[hh][s + 1].start()
            bring(1 + 2 * s, hh)
            bring(2 + 2 * s, hh)
        if s == 0:
            qfar_up.wait_recv()
            share[1, :half, :width] += q_a[...]
            qnear_up.start()
            qfar_dn.wait_recv()
            share[2, half:, :width] += q_b[...]
            qnear_dn.start()
    for hh in range(PARTS):
        fups[hh][3].wait_recv()
        fdowns[hh][3].wait_recv()
        bring(7, hh)
    qnear_up.wait_recv()
    qnear_dn.wait_recv()
    queries[...] = (share[3, :, :width] + q_up[...] + q_dn[...]).astype(queries.dtype)
    for cp in (qfar_up, qfar_dn, qnear_up, qnear_dn):
        cp.wait_send()

    pair = own.shape[-1]
    root = 1.0 / math.sqrt(pair // 2)
    heads = own.shape[2] // near
    ups, downs = [], []
    for hh in range(PARTS):
        ups.append([remote(bg[hh], zp0[hh], zs.at[0, hh], zr.at[0, hh], up),
                    remote(zp0[hh], zp1[hh], zs.at[1, hh], zr.at[1, hh], up),
                    remote(sbuf.at[5, hh], zp2.at[hh, pl.ds(0, 8)], zs.at[2, hh], zr.at[2, hh], up),
                    remote(zp2.at[hh, pl.ds(8, 4)], z4.at[hh, pl.ds(0, 4)], zs.at[3, hh], zr.at[3, hh], up),
                    remote(sbuf.at[7, hh, pl.ds(0, 4)], zp2.at[hh, pl.ds(8, 4)], zs4.at[0, hh], zr4.at[0, hh], up)])
        downs.append([remote(bg[hh], zm0[hh], zs.at[4, hh], zr.at[4, hh], down),
                      remote(zm0[hh], zm1[hh], zs.at[5, hh], zr.at[5, hh], down),
                      remote(sbuf.at[6, hh], zm2.at[hh, pl.ds(0, 8)], zs.at[6, hh], zr.at[6, hh], down),
                      remote(zm2.at[hh, pl.ds(8, 4)], z4.at[hh, pl.ds(4, 4)], zs.at[7, hh], zr.at[7, hh], down),
                      remote(sbuf.at[7, hh, pl.ds(4, 4)], zm2.at[hh, pl.ds(8, 4)], zs4.at[1, hh], zr4.at[1, hh], down)])
    sets = [None, zp0, zm0, zp1, zm1]
    started, gathers = [], []

    def pick(origin, target):
        return (code_ref[origin * 64 + target] // 8) % 16

    def process(k, hh):
        origin = p.dp(0, Z_OFF[k], 0)
        for i, (dy, dc) in enumerate(J_OFF):
            r = pick(origin, p.dp(dy, 0, dc))
            sbuf[k, hh, i] = bg[hh][r] if k == 0 else sets[k][hh][r]
        started.append(plane_send(p, out, k, hh, lambda i: sbuf.at[k, hh, i], ysend, yrecv, ls))

    def forward(k, hh, buf):
        started.append(plane_send(p, out, k, hh, lambda i: buf.at[hh, i], ysend, yrecv, ls))

    def stage(hh, held, place, way, part):
        origin = p.dp(0, -2 * way, 0)
        for i, (dy, dc) in enumerate(J_OFF):
            sbuf[place, hh, i] = held[hh][pick(origin, p.dp(dy, way, dc))]
        for i in range(4):
            dy, dc = J_OFF[part + i]
            sbuf[7, hh, part + i] = held[hh][pick(origin, p.dp(dy, 2 * way, dc))]

    def slot_of(r):
        shard = refs_ref[p.dp(0, 0, 0) * 16 + r] // entries
        dy = (shard // (2 * NZ) + NY - p.y) % NY
        dz = ((shard // 2) % NZ + NZ - p.z) % NZ
        j = jnp.where(dy == 0, 0, jnp.where(dy == 1, 4, jnp.where(dy == 2, 6, 2))) + (shard + p.c) % 2
        return j * 8 + jnp.where(dz < 4, 2 * dz, 2 * NZ - 1 - 2 * dz)

    def attend_part(hh):
        for cp in fsent[hh]:
            cp.wait()

        @pl.loop(0, rows // SPAN // 2)
        def _(step, hh=hh):
            for sub in range(2):
                span = step * 2 + sub
                some = pl.ds(pl.multiple_of(span * SPAN, SPAN), SPAN)
                kv0, kv1 = brought[hh][slot_of(2 * span)], brought[hh][slot_of(2 * span + 1)]
                for i in range(0, heads, 2):
                    first = (hh * heads + i) * (pair // 2)
                    cols = slice(first, first + pair)
                    kv = jnp.concatenate([
                        jnp.concatenate([kv0[h * near:(h + 1) * near], kv1[h * near:(h + 1) * near]], axis=0)
                        for h in (i, i + 1)], axis=1)
                    at, qg, back = attend(queries[some, cols], grads[some, cols], kv, root)
                    attended[some, cols] = at
                    gathered[p.x, some, cols] = qg
                    for h in range(2):
                        lanes = slice(h * pair, (h + 1) * pair)
                        place = slice((i + h) * near, (i + h + 1) * near)
                        bg[hh][2 * span, place, :] = back[:near, lanes]
                        bg[hh][2 * span + 1, place, :] = back[near:, lanes]

        ups[hh][0].start()
        downs[hh][0].start()
        mine = gathered.at[p.x, :, pl.ds(hh * (width // PARTS), width // PARTS)]
        for i, d in enumerate((xup, xdn, xfar)):
            cp = remote(mine, mine, xs.at[i, hh], xr.at[i, hh], d)
            cp.start()
            gathers.append(cp)
        process(0, hh)

    def hop1(hh):
        ups[hh][0].wait_recv()
        ups[hh][1].start()
        downs[hh][0].wait_recv()
        downs[hh][1].start()
        process(1, hh)
        process(2, hh)

    for hh in range(PARTS):
        attend_part(hh)
    for hh in range(PARTS // 2):
        hop1(hh)
    for cp in gathers:
        cp.wait_recv()

    tn = (((0,), (0,)), ((), ()))
    nt = (((1,), (1,)), ((), ()))
    chunk = 32 * NZ
    kept = p.c * chunk
    pairs = []
    for n, dy in enumerate((2, 1, -1, 0)):
        yy = (p.y + dy + NY) % NY

        @pl.loop(0, 2)
        def _(r, yy=yy, n=n):
            cols = pl.ds(pl.multiple_of(r * chunk, chunk), chunk)
            part = lax.dot_general(gathered[yy, :, cols], tokens[...], tn, preferred_element_type=jnp.float32)
            part = part.reshape(NZ // 2, 2, 32, part.shape[1])
            for core in range(2):
                share[n, pl.ds(pl.multiple_of(core * chunk + r * (chunk // 2), chunk // 2), chunk // 2)] = (
                    part[:, core].reshape(chunk // 2, part.shape[3]))

        cp = remote(share.at[n, pl.ds(pl.multiple_of(chunk - kept, chunk), chunk)], crecv.at[n],
                    cs.at[n], cr.at[n], p.dev(0, 0, 1))
        cp.start()
        pairs.append(cp)

    for hh in range(PARTS // 2, PARTS):
        hop1(hh)

    def held(i, count=32):
        return pl.ds(pl.multiple_of(kept + i * 32, 32), count)

    def lump(i):
        return pl.ds(pl.multiple_of(i * 32, 32), 32)

    for n in range(4):
        pairs[n].wait_recv()

        @pl.loop(0, NZ)
        def _(i, n=n):
            share[n, held(i)] += crecv[n, lump(i)]

        if n == 0:
            far_up = remote(share.at[0, held(0, chunk // 2)], y_a, ws.at[0], wr.at[0], yup)
            far_dn = remote(share.at[0, held(4, chunk // 2)], y_b, ws.at[1], wr.at[1], ydn)
            far_up.start()
            far_dn.start()

    @pl.loop(0, 4)
    def _(i):
        some = pl.ds(pl.multiple_of(i * 128, 128), 128)
        total = jnp.zeros((128, weight.shape[0]), jnp.float32)
        for a in range(4):
            total += lax.dot_general(gathered[a, some, :], weight[:, a * 512:(a + 1) * 512], nt,
                                     preferred_element_type=jnp.float32)
        token_grad[some, :] = total.astype(token_grad.dtype)

    far_up.wait_recv()

    @pl.loop(0, 4)
    def _(i):
        share[1, held(i)] += y_a[lump(i)]

    near_up = remote(share.at[1, held(0, chunk)], y_up, ws.at[2], wr.at[2], yup)
    near_up.start()
    far_dn.wait_recv()

    @pl.loop(0, 4)
    def _(i):
        share[2, held(i + 4)] += y_b[lump(i)]

    near_dn = remote(share.at[2, held(0, chunk)], y_dn, ws.at[3], wr.at[3], ydn)
    near_dn.start()

    def hop2(hh):
        ups[hh][1].wait_recv()
        stage(hh, zp1, 5, 1, 0)
        ups[hh][4].start()
        ups[hh][2].start()
        downs[hh][1].wait_recv()
        stage(hh, zm1, 6, -1, 4)
        downs[hh][4].start()
        downs[hh][2].start()
        process(3, hh)
        process(4, hh)

    def hop3(hh):
        ups[hh][4].wait_recv()
        ups[hh][3].start()
        downs[hh][4].wait_recv()
        downs[hh][3].start()
        ups[hh][2].wait_recv()
        forward(5, hh, zp2)
        downs[hh][2].wait_recv()
        forward(6, hh, zm2)

    def hop4(hh):
        ups[hh][3].wait_recv()
        downs[hh][3].wait_recv()
        forward(7, hh, z4)

    for hh in range(PARTS):
        hop2(hh)
    near_up.wait_recv()
    near_dn.wait_recv()

    @pl.loop(0, NZ)
    def _(i):
        s_own[i] = share[3, held(i)] + y_up[lump(i)] + y_dn[lump(i)]

    def at(dz):
        return (p.z + dz + NZ) % NZ

    chain_up = [remote(s_own.at[at(4), pl.ds(0, 16)], w_up1, us.at[0], ur.at[0], up)]
    chain_dn = [remote(s_own.at[at(4), pl.ds(16, 16)], w_dn1, us.at[4], ur.at[4], down)]
    for i, dz in enumerate((3, 2, 1)):
        chain_up.append(remote(s_own.at[at(dz)], w_up.at[i], us.at[1 + i], ur.at[1 + i], up))
        chain_dn.append(remote(s_own.at[at(-dz)], w_dn.at[i], us.at[5 + i], ur.at[5 + i], down))

    def ring(step):
        if step == 1:
            chain_up[0].wait_recv()
            s_own[at(3), pl.ds(0, 16)] += w_up1[...]
            chain_dn[0].wait_recv()
            s_own[at(-3), pl.ds(16, 16)] += w_dn1[...]
        elif step > 1:
            chain_up[step - 1].wait_recv()
            s_own[at(4 - step)] += w_up[step - 2]
            chain_dn[step - 1].wait_recv()
            s_own[at(step - 4)] += w_dn[step - 2]
        if step < 4:
            chain_up[step].start()
            chain_dn[step].start()

    for hh in range(PARTS):
        hop3(hh)
        if hh % (PARTS // 2) == PARTS // 2 - 1:
            ring(hh // (PARTS // 2))
    for hh in range(PARTS):
        hop4(hh)
        if hh % (PARTS // 2) == PARTS // 2 - 1:
            ring(2 + hh // (PARTS // 2))
    chain_up[3].wait_recv()
    chain_dn[3].wait_recv()
    wout[...] = s_own[p.z] + w_up[2] + w_dn[2]

    for local, sends in started:
        local.wait()
        for cp in sends:
            cp.wait()
    for hh in range(PARTS):
        for cp in fups[hh] + fdowns[hh] + ups[hh] + downs[hh]:
            cp.wait_send()
    for cp in gathers + pairs + [far_up, far_dn, near_up, near_dn] + chain_up + chain_dn:
        cp.wait_send()


def whole(near, code, refs_flat, own, tokens, weight, grads):
    n, _, rows, cols = own.shape
    toks, feats = tokens.shape
    width = weight.shape[1] // 4
    low, full = jnp.bfloat16, jnp.float32
    refs = 16
    chunk = 32 * NZ
    blocks = lambda count: [pltpu.VMEM((count, rows, cols), low)] * PARTS
    halves = lambda count: pltpu.VMEM((PARTS, count, rows, cols), low)
    wide = lambda *lead: pltpu.VMEM(lead + (feats,), full)
    flat = lambda count: pltpu.VMEM((count, width), full)
    dma = pltpu.SemaphoreType.DMA
    vmem = pl.BlockSpec(memory_space=pltpu.VMEM)
    smem = pl.BlockSpec(memory_space=pltpu.SMEM)
    hbm = pl.BlockSpec(memory_space=pl.ANY)
    return pl.pallas_call(
        functools.partial(whole_kernel, near),
        out_shape=[
            jax.ShapeDtypeStruct((64, PARTS, rows, cols), low),
            jax.ShapeDtypeStruct((toks, width), low),
            jax.ShapeDtypeStruct((toks, feats), low),
            jax.ShapeDtypeStruct((32, feats), full),
        ],
        in_specs=[smem, smem, vmem, hbm, hbm, hbm],
        out_specs=[hbm, vmem, vmem, vmem],
        scratch_shapes=[blocks(n)] * 7 + [
            pltpu.VMEM((8, PARTS, 8, rows, cols), low),
            blocks(64),
            pltpu.VMEM(tokens.shape, low), pltpu.VMEM(weight.shape, low), pltpu.VMEM(grads.shape, low),
            flat(toks // 2), flat(toks // 2), flat(toks), flat(toks),
            pltpu.VMEM((toks, width), low),
            blocks(refs), blocks(refs), blocks(refs), blocks(refs), blocks(refs),
            halves(12), halves(12), halves(8),
            pltpu.VMEM((4, toks, width), low),
            wide(4, 2 * chunk), wide(4, chunk), wide(NZ, 32),
            wide(chunk // 2), wide(chunk // 2), wide(chunk), wide(chunk),
            wide(16), wide(3, 32), wide(16), wide(3, 32),
            dma((3,)), dma((8, PARTS)), dma((8, PARTS)), dma((8, PARTS, 8)), dma((64, PARTS)), dma((4,)), dma((4,)),
            dma((8, PARTS)), dma((8, PARTS)), dma((2, PARTS)), dma((2, PARTS)),
            dma((8, PARTS, 8)), dma((64, PARTS)), dma((8, PARTS)),
            dma((3, PARTS)), dma((3, PARTS)), dma((4,)), dma((4,)), dma((4,)), dma((4,)), dma((8,)), dma((8,)),
        ],
        compiler_params=pltpu.CompilerParams(
            collective_id=0, has_side_effects=True, vmem_limit_bytes=VMEM_LIMIT),
        cost_estimate=pl.CostEstimate(flops=0, bytes_accessed=500_000_000, transcendentals=0),
        name="whole",
    )(code, refs_flat, own, tokens, weight, grads)


def gather_sum_kernel(code_ref, blk_ref, out_ref, acc):
    p = Place()
    step = pl.program_id(0)

    @pl.when(step == 0)
    def _():
        acc[...] = jnp.zeros_like(acc)

    dy = jnp.where(step == 0, 0, jnp.where(step == 1, -1, jnp.where(step == 2, 1, 2)))
    column = ((p.y + dy + NY) % NY) * (2 * NZ)
    me = p.dp(0, 0, 0)
    for core in range(2):
        for k in range(8):
            source = column + ((p.z + Z_OFF[k] + NZ) % NZ) * 2 + (p.c + core) % 2
            code = code_ref[source * 64 + me]

            @pl.when(code >= 128)
            def _(code=code, i=core * 8 + k):
                e = code % 8
                for h in range(blk_ref.shape[1]):
                    acc[e, h] += blk_ref[i, h].astype(jnp.float32)

    @pl.when(step == 3)
    def _():
        for e in range(8):
            out_ref[e] = jnp.swapaxes(acc[e], 0, 1)


def gather_sum(codes, blocks):
    _, heads, near, pair = blocks.shape
    return pl.pallas_call(
        gather_sum_kernel,
        grid=(4,),
        in_specs=[
            pl.BlockSpec(memory_space=pltpu.SMEM),
            pl.BlockSpec((16, heads, near, pair), lambda i: (i, 0, 0, 0)),
        ],
        out_specs=pl.BlockSpec((8, near, heads, pair), lambda i: (0, 0, 0, 0)),
        out_shape=jax.ShapeDtypeStruct((8, near, heads, pair), jnp.float32),
        scratch_shapes=[pltpu.VMEM((8, heads, near, pair), jnp.float32)],
        compiler_params=pltpu.CompilerParams(vmem_limit_bytes=VMEM_LIMIT),
        name="gather_sum",
    )(codes, blocks)


def on_device(tokens, query_weight, neighbour_store, neighbours, attended_grad):
    entries_here, near, heads, pair = neighbour_store.shape
    flat = neighbours.reshape(-1)
    refs = flat.reshape(64, -1)
    order = jnp.arange(refs.shape[1], dtype=jnp.int32)[None, :]
    word = 128 + 8 * order + refs % entries_here
    shard = jnp.arange(64, dtype=jnp.int32)
    table = jnp.max(
        jnp.where((refs // entries_here)[:, :, None] == shard, word[:, :, None], 0), axis=1)
    code = table.reshape(-1)

    store = neighbour_store.transpose(0, 2, 1, 3).reshape(entries_here, PARTS, heads * near // PARTS, pair)
    back, attended, token_grad, weight_share = whole(
        near, code, flat, store, tokens, query_weight, attended_grad)
    weight_grad = weight_share.T
    store_grad = gather_sum(code, back.reshape(64, heads, near, pair))
    return (attended, token_grad, weight_grad, store_grad)


def solution(mesh):
    return jax.shard_map(
        on_device,
        mesh=mesh,
        in_specs=(
            P("dp", "fsdp"),
            P("fsdp", None),
            P("dp", None, "fsdp", None),
            P(),
            P("dp", "fsdp"),
        ),
        out_specs=(P("dp", "fsdp"), P("dp", "fsdp"), P("fsdp", "dp"), P("dp", None, "fsdp", None)),
        check_vma=False,
    )
```

```python
import functools
import math

import jax
import jax.numpy as jnp
from jax import lax
from jax.experimental import pallas as pl
from jax.experimental.pallas import tpu as pltpu
from jax.sharding import PartitionSpec as P

SPAN = 64
PARTS = 4
NY, NZ = 4, 8
MESH = pl.DeviceIdType.MESH
Z_OFF = (0, -1, 1, -2, 2, -3, 3, 4)
J_OFF = ((0, 0), (0, 1), (-1, 0), (-1, 1), (1, 0), (1, 1), (2, 0), (2, 1))
VMEM_LIMIT = 60 * 1024 * 1024


def dp_of(y, z, c):
    return (y * NZ + z) * 2 + c


class Place:
    def __init__(self):
        me = lax.axis_index("dp")
        self.x = lax.axis_index("fsdp")
        self.y, self.z, self.c = me // (2 * NZ), (me // 2) % NZ, me % 2

    def dp(self, dy, dz, dc):
        return dp_of((self.y + dy + NY) % NY, (self.z + dz + NZ) % NZ, (self.c + dc) % 2)

    def dev(self, dy=0, dz=0, dc=0, dx=0):
        return (self.dp(dy, dz, dc), (self.x + dx + 4) % 4)


def greet(devices):
    barrier = pltpu.get_barrier_semaphore()
    for d in devices:
        pl.semaphore_signal(barrier, inc=1, device_id=d, device_id_type=MESH)
    pl.semaphore_wait(barrier, len(devices))


def remote(src, dst, ssem, rsem, d):
    return pltpu.make_async_remote_copy(
        src_ref=src, dst_ref=dst, send_sem=ssem, recv_sem=rsem, device_id=d, device_id_type=MESH)


def drain(ref, sem):
    pltpu.make_async_copy(ref, ref, sem).wait()


def plane_partners(p):
    return [p.dev(dy, 0, dc) for dy, dc in J_OFF[1:]]


SLOTS = ((1, 1), (6, 6), (7, 7), (4, 2), (5, 3), (2, 4), (3, 5))


def plane_send(p, out, k, hh, blocks, ysend, yrecv, ls):
    pltpu.make_async_copy(blocks(0), out.at[k, hh], ls).start()
    for i, j in SLOTS:
        dy, dc = J_OFF[i]
        remote(blocks(i), out.at[j * 8 + k, hh], ysend, yrecv, p.dev(dy, 0, dc)).start()


def attend(q, g, kv, root):
    pair = q.shape[1]
    width = pair // 2
    left = lax.broadcasted_iota(jnp.int32, q.shape, 1) < width
    zero = jnp.zeros(q.shape, q.dtype)

    def dot(a, b, dims):
        return lax.dot_general(a, b, (dims, ((), ())), preferred_element_type=jnp.float32)

    def swap(a):
        return jnp.concatenate([a[:, width:], a[:, :width]], axis=1)

    def row(a, b):
        return jnp.concatenate([a, b], axis=1)

    both = jnp.concatenate([
        row(jnp.where(left, q, zero), zero),
        row(zero, jnp.where(left, swap(q), zero)),
        row(jnp.where(left, zero, swap(g)), zero),
        row(zero, jnp.where(left, zero, g)),
    ], axis=0)
    raw = dot(kv, both, ((1,), (1,)))
    score = raw[:, :pair] * root
    prob_grad = raw[:, pair:]
    weights = jnp.exp(score - jnp.max(score, axis=0, keepdims=True))
    probs = weights / jnp.sum(weights, axis=0, keepdims=True)
    low = probs.astype(jnp.bfloat16)
    term = jnp.sum(probs * prob_grad, axis=0, keepdims=True)
    sg = (probs * (prob_grad - term)).astype(jnp.bfloat16)
    applied = dot(row(low, sg), kv, ((0,), (0,)))
    at_a, at_b = applied[:SPAN, :pair], applied[SPAN:2 * SPAN, pair:]
    qg_a, qg_b = applied[2 * SPAN:3 * SPAN, :pair], applied[3 * SPAN:, pair:]
    attended = jnp.where(left, swap(at_a), at_b).astype(jnp.bfloat16)
    query_grad = (jnp.where(left, qg_a, swap(qg_b)) * root).astype(jnp.bfloat16)
    back = dot(row(sg, low), both, ((1,), (0,)))
    scale = jnp.where(lax.broadcasted_iota(jnp.int32, back.shape, 1) % pair < width, root, 1.0)
    return attended, query_grad, (back * scale).astype(jnp.bfloat16)


def whole_kernel(near, code_ref, refs_ref, own, tokens_far, weight_far, grads_far,
                 out, attended, token_grad, wout,
                 fp0, fp1, fp2, fm0, fm1, fm2, f4, sbuf, brought, tokens, weight, grads,
                 q_a, q_b, q_up, q_dn, queries, bg,
                 zp0, zp1, zm0, zm1, zp2, zm2, z4, gathered, share, crecv, s_own,
                 y_a, y_b, y_up, y_dn, w_up1, w_up, w_dn1, w_dn,
                 fetch, fs, fr, fysend, fyrecv, qs, qr,
                 zs, zr, zs4, zr4, ysend, yrecv, ls, xs, xr, cs, cr, ws, wr, us, ur):
    p = Place()
    fetches = [pltpu.make_async_copy(tokens_far, tokens, fetch.at[0]),
               pltpu.make_async_copy(weight_far, weight, fetch.at[1]),
               pltpu.make_async_copy(grads_far, grads, fetch.at[2])]
    for cp in fetches:
        cp.start()
    up, down = p.dev(0, 1), p.dev(0, -1)
    yup, ydn = p.dev(1), p.dev(-1)
    xup, xdn, xfar = p.dev(dx=1), p.dev(dx=-1), p.dev(dx=2)
    greet([up, down, xup, xdn, xfar] + plane_partners(p))

    entries = own.shape[0]
    lo, hi = pl.ds(0, entries // 2), pl.ds(entries // 2, entries // 2)
    fups, fdowns = [], []
    for hh in range(PARTS):
        fups.append([remote(own.at[:, hh], fp0[hh], fs.at[0, hh], fr.at[0, hh], up),
                     remote(fp0[hh], fp1[hh], fs.at[1, hh], fr.at[1, hh], up),
                     remote(fp1[hh], fp2[hh], fs.at[2, hh], fr.at[2, hh], up),
                     remote(fp2[hh].at[lo], f4[hh].at[lo], fs.at[3, hh], fr.at[3, hh], up)])
        fdowns.append([remote(own.at[:, hh], fm0[hh], fs.at[4, hh], fr.at[4, hh], down),
                       remote(fm0[hh], fm1[hh], fs.at[5, hh], fr.at[5, hh], down),
                       remote(fm1[hh], fm2[hh], fs.at[6, hh], fr.at[6, hh], down),
                       remote(fm2[hh].at[hi], f4[hh].at[hi], fs.at[7, hh], fr.at[7, hh], down)])
    fsets = [None, fp0, fm0, fp1, fm1, fp2, fm2, f4]

    def bring(k, hh):
        origin = p.dp(0, Z_OFF[k], 0)

        def block(i):
            dy, dc = J_OFF[i]
            e = code_ref[p.dp(dy, 0, dc) * 64 + origin] % 8
            return own[e, hh] if k == 0 else fsets[k][hh][e]

        brought[hh][k] = block(0)
        for i, j in SLOTS:
            dy, dc = J_OFF[i]
            sbuf[k, hh, i] = block(i)
            remote(sbuf.at[k, hh, i], brought[hh].at[j * 8 + k], fysend.at[hh],
                   fyrecv.at[hh], p.dev(dy, 0, dc)).start()

    for hh in range(PARTS):
        fups[hh][0].start()
        fdowns[hh][0].start()
    for hh in range(PARTS):
        bring(0, hh)

    for cp in fetches:
        cp.wait()
    rows, width = queries.shape
    half = rows // 2
    parts = [share.at[n, :, pl.ds(0, width)] for n in range(4)]
    for n, dx in enumerate((2, 1, -1, 0)):
        cols = pl.ds(pl.multiple_of((p.x + dx + 4) % 4 * width, width), width)

        @pl.loop(0, 4)
        def _(r, n=n, cols=cols):
            some = pl.ds(pl.multiple_of(r * (rows // 4), rows // 4), rows // 4)
            share[n, some, :width] = jnp.dot(
                tokens[some, :], weight[:, cols], preferred_element_type=jnp.float32)

        if n == 0:
            qfar_up = remote(share.at[0, pl.ds(0, half), pl.ds(0, width)], q_a, qs.at[0], qr.at[0], xup)
            qfar_dn = remote(share.at[0, pl.ds(half, half), pl.ds(0, width)], q_b, qs.at[1], qr.at[1], xdn)
            qfar_up.start()
            qfar_dn.start()

    qnear_up = remote(parts[1], q_up, qs.at[2], qr.at[2], xup)
    qnear_dn = remote(parts[2], q_dn, qs.at[3], qr.at[3], xdn)
    for s in range(3):
        for hh in range(PARTS):
            fups[hh][s].wait_recv()
            fups[hh][s + 1].start()
            fdowns[hh][s].wait_recv()
            fdowns[hh][s + 1].start()
            bring(1 + 2 * s, hh)
            bring(2 + 2 * s, hh)
        if s == 0:
            qfar_up.wait_recv()
            share[1, :half, :width] += q_a[...]
            qnear_up.start()
            qfar_dn.wait_recv()
            share[2, half:, :width] += q_b[...]
            qnear_dn.start()
    for hh in range(PARTS):
        fups[hh][3].wait_recv()
        fdowns[hh][3].wait_recv()
        bring(7, hh)
    qnear_up.wait_recv()
    qnear_dn.wait_recv()
    queries[...] = (share[3, :, :width] + q_up[...] + q_dn[...]).astype(queries.dtype)
    for cp in (qfar_up, qfar_dn, qnear_up, qnear_dn):
        cp.wait_send()

    pair = own.shape[-1]
    root = 1.0 / math.sqrt(pair // 2)
    heads = own.shape[2] // near
    ups, downs = [], []
    for hh in range(PARTS):
        ups.append([remote(bg[hh], zp0[hh], zs.at[0, hh], zr.at[0, hh], up),
                    remote(zp0[hh], zp1[hh], zs.at[1, hh], zr.at[1, hh], up),
                    remote(sbuf.at[5, hh], zp2.at[hh, pl.ds(0, 8)], zs.at[2, hh], zr.at[2, hh], up),
                    remote(zp2.at[hh, pl.ds(8, 4)], z4.at[hh, pl.ds(0, 4)], zs.at[3, hh], zr.at[3, hh], up),
                    remote(sbuf.at[7, hh, pl.ds(0, 4)], zp2.at[hh, pl.ds(8, 4)], zs4.at[0, hh], zr4.at[0, hh], up)])
        downs.append([remote(bg[hh], zm0[hh], zs.at[4, hh], zr.at[4, hh], down),
                      remote(zm0[hh], zm1[hh], zs.at[5, hh], zr.at[5, hh], down),
                      remote(sbuf.at[6, hh], zm2.at[hh, pl.ds(0, 8)], zs.at[6, hh], zr.at[6, hh], down),
                      remote(zm2.at[hh, pl.ds(8, 4)], z4.at[hh, pl.ds(4, 4)], zs.at[7, hh], zr.at[7, hh], down),
                      remote(sbuf.at[7, hh, pl.ds(4, 4)], zm2.at[hh, pl.ds(8, 4)], zs4.at[1, hh], zr4.at[1, hh], down)])
    sets = [None, zp0, zm0, zp1, zm1]
    gathers = []

    def pick(origin, target):
        return (code_ref[origin * 64 + target] // 8) % 16

    def process(k, hh):
        origin = p.dp(0, Z_OFF[k], 0)
        for i, (dy, dc) in enumerate(J_OFF):
            r = pick(origin, p.dp(dy, 0, dc))
            sbuf[k, hh, i] = bg[hh][r] if k == 0 else sets[k][hh][r]
        plane_send(p, out, k, hh, lambda i: sbuf.at[k, hh, i], ysend, yrecv, ls)

    def forward(k, hh, buf):
        plane_send(p, out, k, hh, lambda i: buf.at[hh, i], ysend, yrecv, ls)

    def stage(hh, held, place, way, part):
        origin = p.dp(0, -2 * way, 0)
        for i, (dy, dc) in enumerate(J_OFF):
            sbuf[place, hh, i] = held[hh][pick(origin, p.dp(dy, way, dc))]
        for i in range(4):
            dy, dc = J_OFF[part + i]
            sbuf[7, hh, part + i] = held[hh][pick(origin, p.dp(dy, 2 * way, dc))]

    def slot_of(r):
        shard = refs_ref[p.dp(0, 0, 0) * 16 + r] // entries
        dy = (shard // (2 * NZ) + NY - p.y) % NY
        dz = ((shard // 2) % NZ + NZ - p.z) % NZ
        j = jnp.where(dy == 0, 0, jnp.where(dy == 1, 4, jnp.where(dy == 2, 6, 2))) + (shard + p.c) % 2
        return j * 8 + jnp.where(dz < 4, 2 * dz, 2 * NZ - 1 - 2 * dz)

    def attend_part(hh):
        drain(brought[hh].at[pl.ds(8, 56)], fyrecv.at[hh])
        drain(brought[hh].at[pl.ds(8, 56)], fysend.at[hh])

        @pl.loop(0, rows // SPAN // 2)
        def _(step, hh=hh):
            for sub in range(2):
                span = step * 2 + sub
                some = pl.ds(pl.multiple_of(span * SPAN, SPAN), SPAN)
                kv0, kv1 = brought[hh][slot_of(2 * span)], brought[hh][slot_of(2 * span + 1)]
                for i in range(0, heads, 2):
                    first = (hh * heads + i) * (pair // 2)
                    cols = slice(first, first + pair)
                    kv = jnp.concatenate([
                        jnp.concatenate([kv0[h * near:(h + 1) * near], kv1[h * near:(h + 1) * near]], axis=0)
                        for h in (i, i + 1)], axis=1)
                    at, qg, back = attend(queries[some, cols], grads[some, cols], kv, root)
                    attended[some, cols] = at
                    gathered[p.x, some, cols] = qg
                    for h in range(2):
                        lanes = slice(h * pair, (h + 1) * pair)
                        place = slice((i + h) * near, (i + h + 1) * near)
                        bg[hh][2 * span, place, :] = back[:near, lanes]
                        bg[hh][2 * span + 1, place, :] = back[near:, lanes]

        ups[hh][0].start()
        downs[hh][0].start()
        mine = gathered.at[p.x, :, pl.ds(hh * (width // PARTS), width // PARTS)]
        for i, d in enumerate((xup, xdn, xfar)):
            cp = remote(mine, mine, xs.at[i, hh], xr.at[i, hh], d)
            cp.start()
            gathers.append(cp)
        process(0, hh)

    def hop1(hh):
        ups[hh][0].wait_recv()
        ups[hh][1].start()
        downs[hh][0].wait_recv()
        downs[hh][1].start()
        process(1, hh)
        process(2, hh)

    for hh in range(PARTS):
        attend_part(hh)
    for hh in range(PARTS // 2):
        hop1(hh)
    for cp in gathers:
        cp.wait_recv()

    tn = (((0,), (0,)), ((), ()))
    nt = (((1,), (1,)), ((), ()))
    chunk = 32 * NZ
    kept = p.c * chunk
    pairs = []
    for n, dy in enumerate((2, 1, -1, 0)):
        yy = (p.y + dy + NY) % NY

        @pl.loop(0, 2)
        def _(r, yy=yy, n=n):
            cols = pl.ds(pl.multiple_of(r * chunk, chunk), chunk)
            part = lax.dot_general(gathered[yy, :, cols], tokens[...], tn, preferred_element_type=jnp.float32)
            part = part.reshape(NZ // 2, 2, 32, part.shape[1])
            for core in range(2):
                share[n, pl.ds(pl.multiple_of(core * chunk + r * (chunk // 2), chunk // 2), chunk // 2)] = (
                    part[:, core].reshape(chunk // 2, part.shape[3]))

        cp = remote(share.at[n, pl.ds(pl.multiple_of(chunk - kept, chunk), chunk)], crecv.at[n],
                    cs.at[n], cr.at[n], p.dev(0, 0, 1))
        cp.start()
        pairs.append(cp)

    for hh in range(PARTS // 2, PARTS):
        hop1(hh)

    def held(i, count=32):
        return pl.ds(pl.multiple_of(kept + i * 32, 32), count)

    def lump(i):
        return pl.ds(pl.multiple_of(i * 32, 32), 32)

    for n in range(4):
        pairs[n].wait_recv()

        @pl.loop(0, NZ)
        def _(i, n=n):
            share[n, held(i)] += crecv[n, lump(i)]

        if n == 0:
            far_up = remote(share.at[0, held(0, chunk // 2)], y_a, ws.at[0], wr.at[0], yup)
            far_dn = remote(share.at[0, held(4, chunk // 2)], y_b, ws.at[1], wr.at[1], ydn)
            far_up.start()
            far_dn.start()

    @pl.loop(0, 4)
    def _(i):
        some = pl.ds(pl.multiple_of(i * 128, 128), 128)
        total = jnp.zeros((128, weight.shape[0]), jnp.float32)
        for a in range(4):
            total += lax.dot_general(gathered[a, some, :], weight[:, a * 512:(a + 1) * 512], nt,
                                     preferred_element_type=jnp.float32)
        token_grad[some, :] = total.astype(token_grad.dtype)

    far_up.wait_recv()

    @pl.loop(0, 4)
    def _(i):
        share[1, held(i)] += y_a[lump(i)]

    near_up = remote(share.at[1, held(0, chunk)], y_up, ws.at[2], wr.at[2], yup)
    near_up.start()
    far_dn.wait_recv()

    @pl.loop(0, 4)
    def _(i):
        share[2, held(i + 4)] += y_b[lump(i)]

    near_dn = remote(share.at[2, held(0, chunk)], y_dn, ws.at[3], wr.at[3], ydn)
    near_dn.start()

    def hop2(hh):
        ups[hh][1].wait_recv()
        stage(hh, zp1, 5, 1, 0)
        ups[hh][4].start()
        ups[hh][2].start()
        downs[hh][1].wait_recv()
        stage(hh, zm1, 6, -1, 4)
        downs[hh][4].start()
        downs[hh][2].start()
        process(3, hh)
        process(4, hh)

    def hop3(hh):
        ups[hh][4].wait_recv()
        ups[hh][3].start()
        downs[hh][4].wait_recv()
        downs[hh][3].start()
        ups[hh][2].wait_recv()
        forward(5, hh, zp2)
        downs[hh][2].wait_recv()
        forward(6, hh, zm2)

    def hop4(hh):
        ups[hh][3].wait_recv()
        downs[hh][3].wait_recv()
        forward(7, hh, z4)

    for hh in range(PARTS):
        hop2(hh)
    near_up.wait_recv()
    near_dn.wait_recv()

    @pl.loop(0, NZ)
    def _(i):
        s_own[i] = share[3, held(i)] + y_up[lump(i)] + y_dn[lump(i)]

    def at(dz):
        return (p.z + dz + NZ) % NZ

    chain_up = [remote(s_own.at[at(4), pl.ds(0, 16)], w_up1, us.at[0], ur.at[0], up)]
    chain_dn = [remote(s_own.at[at(4), pl.ds(16, 16)], w_dn1, us.at[4], ur.at[4], down)]
    for i, dz in enumerate((3, 2, 1)):
        chain_up.append(remote(s_own.at[at(dz)], w_up.at[i], us.at[1 + i], ur.at[1 + i], up))
        chain_dn.append(remote(s_own.at[at(-dz)], w_dn.at[i], us.at[5 + i], ur.at[5 + i], down))

    def ring(step):
        if step == 1:
            chain_up[0].wait_recv()
            s_own[at(3), pl.ds(0, 16)] += w_up1[...]
            chain_dn[0].wait_recv()
            s_own[at(-3), pl.ds(16, 16)] += w_dn1[...]
        elif step > 1:
            chain_up[step - 1].wait_recv()
            s_own[at(4 - step)] += w_up[step - 2]
            chain_dn[step - 1].wait_recv()
            s_own[at(step - 4)] += w_dn[step - 2]
        if step < 4:
            chain_up[step].start()
            chain_dn[step].start()

    for hh in range(PARTS):
        hop3(hh)
        if hh % (PARTS // 2) == PARTS // 2 - 1:
            ring(hh // (PARTS // 2))
    for hh in range(PARTS):
        hop4(hh)
        if hh % (PARTS // 2) == PARTS // 2 - 1:
            ring(2 + hh // (PARTS // 2))
    chain_up[3].wait_recv()
    chain_dn[3].wait_recv()
    wout[...] = s_own[p.z] + w_up[2] + w_dn[2]

    drain(out.at[pl.ds(0, 8)], ls)
    drain(out.at[pl.ds(8, 56)], ysend)
    drain(out.at[pl.ds(8, 56)], yrecv)
    for hh in range(PARTS):
        for cp in fups[hh] + fdowns[hh] + ups[hh] + downs[hh]:
            cp.wait_send()
    for cp in gathers + pairs + [far_up, far_dn, near_up, near_dn] + chain_up + chain_dn:
        cp.wait_send()


def whole(near, code, refs_flat, own, tokens, weight, grads):
    n, _, rows, cols = own.shape
    toks, feats = tokens.shape
    width = weight.shape[1] // 4
    low, full = jnp.bfloat16, jnp.float32
    refs = 16
    chunk = 32 * NZ
    blocks = lambda count: [pltpu.VMEM((count, rows, cols), low)] * PARTS
    halves = lambda count: pltpu.VMEM((PARTS, count, rows, cols), low)
    wide = lambda *lead: pltpu.VMEM(lead + (feats,), full)
    flat = lambda count: pltpu.VMEM((count, width), full)
    dma = pltpu.SemaphoreType.DMA
    vmem = pl.BlockSpec(memory_space=pltpu.VMEM)
    smem = pl.BlockSpec(memory_space=pltpu.SMEM)
    hbm = pl.BlockSpec(memory_space=pl.ANY)
    return pl.pallas_call(
        functools.partial(whole_kernel, near),
        out_shape=[
            jax.ShapeDtypeStruct((64, PARTS, rows, cols), low),
            jax.ShapeDtypeStruct((toks, width), low),
            jax.ShapeDtypeStruct((toks, feats), low),
            jax.ShapeDtypeStruct((32, feats), full),
        ],
        in_specs=[smem, smem, vmem, hbm, hbm, hbm],
        out_specs=[hbm, vmem, vmem, vmem],
        scratch_shapes=[blocks(n)] * 7 + [
            pltpu.VMEM((8, PARTS, 8, rows, cols), low),
            blocks(64),
            pltpu.VMEM(tokens.shape, low), pltpu.VMEM(weight.shape, low), pltpu.VMEM(grads.shape, low),
            flat(toks // 2), flat(toks // 2), flat(toks), flat(toks),
            pltpu.VMEM((toks, width), low),
            blocks(refs), blocks(refs), blocks(refs), blocks(refs), blocks(refs),
            halves(12), halves(12), halves(8),
            pltpu.VMEM((4, toks, width), low),
            wide(4, 2 * chunk), wide(4, chunk), wide(NZ, 32),
            wide(chunk // 2), wide(chunk // 2), wide(chunk), wide(chunk),
            wide(16), wide(3, 32), wide(16), wide(3, 32),
            dma((3,)), dma((8, PARTS)), dma((8, PARTS)), dma((PARTS,)), dma((PARTS,)), dma((4,)), dma((4,)),
            dma((8, PARTS)), dma((8, PARTS)), dma((2, PARTS)), dma((2, PARTS)),
            dma, dma, dma,
            dma((3, PARTS)), dma((3, PARTS)), dma((4,)), dma((4,)), dma((4,)), dma((4,)), dma((8,)), dma((8,)),
        ],
        compiler_params=pltpu.CompilerParams(
            collective_id=0, has_side_effects=True, vmem_limit_bytes=VMEM_LIMIT),
        cost_estimate=pl.CostEstimate(flops=0, bytes_accessed=500_000_000, transcendentals=0),
        name="whole",
    )(code, refs_flat, own, tokens, weight, grads)


def gather_sum_kernel(code_ref, blk_ref, out_ref, acc):
    p = Place()
    step = pl.program_id(0)

    @pl.when(step == 0)
    def _():
        acc[...] = jnp.zeros_like(acc)

    dy = jnp.where(step == 0, 0, jnp.where(step == 1, -1, jnp.where(step == 2, 1, 2)))
    column = ((p.y + dy + NY) % NY) * (2 * NZ)
    me = p.dp(0, 0, 0)
    for core in range(2):
        for k in range(8):
            source = column + ((p.z + Z_OFF[k] + NZ) % NZ) * 2 + (p.c + core) % 2
            code = code_ref[source * 64 + me]

            @pl.when(code >= 128)
            def _(code=code, i=core * 8 + k):
                e = code % 8
                for h in range(blk_ref.shape[1]):
                    acc[e, h] += blk_ref[i, h].astype(jnp.float32)

    @pl.when(step == 3)
    def _():
        for e in range(8):
            out_ref[e] = jnp.swapaxes(acc[e], 0, 1)


def gather_sum(codes, blocks):
    _, heads, near, pair = blocks.shape
    return pl.pallas_call(
        gather_sum_kernel,
        grid=(4,),
        in_specs=[
            pl.BlockSpec(memory_space=pltpu.SMEM),
            pl.BlockSpec((16, heads, near, pair), lambda i: (i, 0, 0, 0)),
        ],
        out_specs=pl.BlockSpec((8, near, heads, pair), lambda i: (0, 0, 0, 0)),
        out_shape=jax.ShapeDtypeStruct((8, near, heads, pair), jnp.float32),
        scratch_shapes=[pltpu.VMEM((8, heads, near, pair), jnp.float32)],
        compiler_params=pltpu.CompilerParams(vmem_limit_bytes=VMEM_LIMIT),
        name="gather_sum",
    )(codes, blocks)


def on_device(tokens, query_weight, neighbour_store, neighbours, attended_grad):
    entries_here, near, heads, pair = neighbour_store.shape
    flat = neighbours.reshape(-1)
    refs = flat.reshape(64, -1)
    order = jnp.arange(refs.shape[1], dtype=jnp.int32)[None, :]
    word = 128 + 8 * order + refs % entries_here
    shard = jnp.arange(64, dtype=jnp.int32)
    table = jnp.max(
        jnp.where((refs // entries_here)[:, :, None] == shard, word[:, :, None], 0), axis=1)
    code = table.reshape(-1)

    store = neighbour_store.transpose(0, 2, 1, 3).reshape(entries_here, PARTS, heads * near // PARTS, pair)
    back, attended, token_grad, weight_share = whole(
        near, code, flat, store, tokens, query_weight, attended_grad)
    weight_grad = weight_share.T
    store_grad = gather_sum(code, back.reshape(64, heads, near, pair))
    return (attended, token_grad, weight_grad, store_grad)


def solution(mesh):
    return jax.shard_map(
        on_device,
        mesh=mesh,
        in_specs=(
            P("dp", "fsdp"),
            P("fsdp", None),
            P("dp", None, "fsdp", None),
            P(),
            P("dp", "fsdp"),
        ),
        out_specs=(P("dp", "fsdp"), P("dp", "fsdp"), P("fsdp", "dp"), P("dp", None, "fsdp", None)),
        check_vma=False,
    )
```
